128 devices in a mesh: batch: 16 (over y, x), proto: 8 (over z, core).
Axes of the slice: x: 4, y: 4, z: 4, core: 2. Of those that a mesh axis runs over, the one named last changes fastest.
Arguments:
- teacher_emb: bfloat16 [16384, 256], P('batch'), may hold values from -24 to 24
- student_emb: bfloat16 [16384, 256], P('batch'), may hold values from -24 to 24
- prototypes: bfloat16 [256, 65536], P(None, 'proto'), may hold values from -2 to 2
Outputs:
- crop_loss: float32 [16384], P('batch')
- proto_grad: float32 [256, 65536], P('batch', 'proto')
The draws below stay inside these ranges and needn't reach their ends.
All inputs are finite; a program needn't handle non-finite values.
Results may differ from the reference program's by a relative error of at most 0.0085.
Values sent between devices are 32-bit elements; how exact they have to be, the bound alone decides.
A program may use at most 192 MiB of HBM per device.

```python
import math
import jax
import jax.numpy as jnp
from jax import lax

D = 256
PROTOS = 65536
ITERS = 3
CROPS = 16384
N_PROTO = 8


def shared_layout(key):
    key_centers, key_crops, key_groups = jax.random.split(key, 3)
    centers = jnp.clip(jax.random.normal(key_centers, (8, D), jnp.float32), -4.0, 4.0)
    ticket = jax.random.randint(key_crops, (CROPS,), 0, 36)
    bounds = jnp.array([1, 3, 6, 10, 15, 21, 28], jnp.int32)
    crop_group = jnp.sum((ticket[:, None] >= bounds[None, :]).astype(jnp.int32), axis=1)
    crop_group = jnp.sort(crop_group)
    proto_group = jax.random.randint(key_groups, (PROTOS,), 0, 8)
    return (centers, crop_group, proto_group)


def draw_teacher_emb(key, part):
    centers, crop_group, unused = shared_layout(key)
    key = jax.random.fold_in(key, 11)
    key_noise = jax.random.fold_in(key, 0)
    base = jnp.take(centers, crop_group, axis=0)
    noise = jnp.clip(jax.random.normal(key_noise, (CROPS, D), jnp.float32), -4.0, 4.0)
    values = base + noise
    return values.astype(jnp.bfloat16)


def draw_student_emb(key, part):
    centers, crop_group, unused = shared_layout(key)
    key = jax.random.fold_in(key, 23)
    key_noise = jax.random.fold_in(key, 0)
    base = jnp.take(centers, crop_group, axis=0)
    noise = jnp.clip(jax.random.normal(key_noise, (CROPS, D), jnp.float32), -4.0, 4.0)
    values = base + noise
    return values.astype(jnp.bfloat16)


def draw_prototypes(key, part):
    centers, unused, proto_group = shared_layout(key)
    key = jax.random.fold_in(key, 37)
    key_noise = jax.random.fold_in(key, 0)
    base = jnp.take(centers, proto_group, axis=0).T
    noise = jnp.clip(jax.random.normal(key_noise, (D, PROTOS), jnp.float32), -4.0, 4.0)
    values = 0.05 * (base + noise)
    return values.astype(jnp.bfloat16)


def setup_inputs(seed: int = 0) -> dict:
    key_of = jax.random.split(jax.random.key(seed), 4)
    teacher_emb = draw_teacher_emb(jax.random.fold_in(key_of[3], 71), 0)
    student_emb = draw_student_emb(jax.random.fold_in(key_of[3], 71), 0)
    prototypes = draw_prototypes(jax.random.fold_in(key_of[3], 71), 0)
    return dict(teacher_emb=teacher_emb, student_emb=student_emb, prototypes=prototypes)


TEACHER_TEMP = 0.07
STUDENT_TEMP = 0.1

def unit_rows(values, axis):
    wide = values.astype(jnp.float32)
    return (wide * lax.rsqrt(lax.optimization_barrier(jnp.sum(wide * wide, axis=axis, keepdims=True)) + 1e-06)).astype(jnp.bfloat16)

def reference(teacher_emb, student_emb, prototypes):
    unit_teacher = unit_rows(teacher_emb, 1)
    unit_student = unit_rows(student_emb, 1)
    unit_protos = unit_rows(prototypes, 0)
    block_count = N_PROTO
    block_width = PROTOS // N_PROTO
    weight_blocks = unit_protos.reshape(D, block_count, block_width).transpose(1, 0, 2)
    offset = jnp.zeros((CROPS,), jnp.float32)
    start_sum = jnp.zeros((CROPS,), jnp.float32)
    shift_blocks = None
    for sweep_index in range(ITERS):

        def sweep_step(running_sum, weight_block):
            scores = jnp.dot(unit_teacher, weight_block, preferred_element_type=jnp.float32) / TEACHER_TEMP
            col_sum = lax.optimization_barrier(jnp.sum(jnp.exp(scores + offset[:, None]), axis=0))
            shift_block = -math.log(PROTOS) - jnp.log(col_sum)
            new_sum = running_sum + lax.optimization_barrier(jnp.sum(jnp.exp(scores + shift_block[None, :]), axis=1))
            return (new_sum, shift_block)
        row_sum, shift_blocks = lax.scan(sweep_step, start_sum, weight_blocks)
        offset = -math.log(CROPS) - jnp.log(row_sum)

    def student_step(running_sum, weight_block):
        scores = jnp.dot(unit_student, weight_block, preferred_element_type=jnp.float32) / STUDENT_TEMP
        return (running_sum + lax.optimization_barrier(jnp.sum(jnp.exp(scores), axis=1)), None)
    s_sum, unused = lax.scan(student_step, start_sum, weight_blocks)
    log_total = jnp.log(s_sum)
    factor = PROTOS / (STUDENT_TEMP * CROPS)

    def final_step(cross, inputs):
        weight_block, shift_block = inputs
        teacher = jnp.dot(unit_teacher, weight_block, preferred_element_type=jnp.float32) / TEACHER_TEMP
        student = jnp.dot(unit_student, weight_block, preferred_element_type=jnp.float32) / STUDENT_TEMP
        target = jnp.exp(teacher + shift_block[None, :] + offset[:, None] + math.log(CROPS))
        student_prob = jnp.exp(student - log_total[:, None])
        cross = cross + lax.optimization_barrier(jnp.sum(target * student, axis=1))
        grad_scaled = ((student_prob - target) * factor).astype(jnp.bfloat16)
        grad_block = lax.dot_general(unit_student, grad_scaled, (((0,), (0,)), ((), ())), preferred_element_type=jnp.float32)
        return (cross, grad_block)
    cross, grad_blocks = lax.scan(final_step, jnp.zeros((CROPS,), jnp.float32), (weight_blocks, shift_blocks))
    crop_loss = log_total - cross
    proto_grad = grad_blocks.transpose(1, 0, 2).reshape(D, PROTOS)
    return (crop_loss, proto_grad)
```

```python
import functools
import math

import jax
import jax.numpy as jnp
from jax import lax
from jax.experimental import pallas as pl
from jax.experimental.pallas import tpu as pltpu
from jax.sharding import PartitionSpec as P

PROTOS = 65536
CROPS = 16384
ITERS = 3
TEACHER_TEMP = 0.07
STUDENT_TEMP = 0.1
NB = 16
NP = 8
ROWS = 1024
COLS = 8192
D = 256
LOG2E = 1.4426950408889634
MESH = pl.DeviceIdType.MESH
F32 = jnp.float32
BF16 = jnp.bfloat16


def unit(values, axis):
    wide = values.astype(F32)
    return (wide * lax.rsqrt(jnp.sum(wide * wide, axis=axis, keepdims=True) + 1e-06)).astype(BF16)


def rows_to_vec(part):
    out = []
    for i in range(8):
        block = part[pl.ds(i * 128, 128), :]
        out.append(jnp.sum(block.T, axis=0, keepdims=True))
    return jnp.concatenate(out, axis=0)


def vec_to_rows(vec, out):
    for i in range(8):
        out[pl.ds(i * 128, 128), :] = jnp.broadcast_to(vec[i : i + 1, :], (128, 128)).T


def kernel(
    te, se, pr, loss, grad,
    ut, us, ust, up, big, part, wide, col, col_in, cvec, rvec, row_in, gbuf, zvec, z_in, xvec, x_in,
    s_col, r_col, s_c, r_c, s_row, r_row,
):
    mb = lax.axis_index("batch")
    mp = lax.axis_index("proto")
    barrier = pltpu.get_barrier_semaphore()

    def greet_batch(d, carry):
        pl.semaphore_signal(barrier, inc=1, device_id={"batch": lax.rem(mb + d, NB)}, device_id_type=MESH)
        return carry

    def greet_proto(d, carry):
        pl.semaphore_signal(barrier, inc=1, device_id={"proto": lax.rem(mp + d, NP)}, device_id_type=MESH)
        return carry

    lax.fori_loop(1, NB, greet_batch, 0)
    lax.fori_loop(1, NP, greet_proto, 0)

    ut[...] = unit(te[...], 1)
    us[...] = unit(se[...], 1)
    for i in range(8):
        block = us[pl.ds(i * 128, 128), :]
        ust[:, pl.ds(i * 128, 128)] = block.astype(F32).T.astype(BF16)

    def first(j, carry):
        cols = pl.ds(pl.multiple_of(j * 512, 512), 512)
        w = unit(pr[:, cols], 0)
        up[:, cols] = w
        total = jnp.zeros((8, 512), F32)
        for i in range(4):
            rows = pl.ds(i * 256, 256)
            e = jnp.exp2(jnp.dot(ut[rows, :], w, preferred_element_type=F32) * (LOG2E / TEACHER_TEMP))
            big[rows, cols] = e
            total = total + jnp.sum(e.reshape(32, 8, 512), axis=0)
        flat = jnp.sum(total, axis=0, keepdims=True)
        for k in range(4):
            col[0, j, pl.ds(k, 1), :] = flat[:, k * 128 : (k + 1) * 128]
        return carry

    lax.fori_loop(0, 16, first, 0)
    pl.semaphore_wait(barrier, NB + NP - 2)

    def sum_cols(it):
        def send(d, carry):
            to = lax.rem(mb + d, NB)
            pltpu.make_async_remote_copy(
                src_ref=col.at[it, to], dst_ref=col_in.at[it, mb],
                send_sem=s_col.at[it], recv_sem=r_col.at[it],
                device_id={"batch": to}, device_id_type=MESH,
            ).start()
            return carry

        lax.fori_loop(1, NB, send, 0)
        col_in[it, mb] = col[it, mb]
        some = col_in.at[it, pl.ds(0, NB - 1)]
        pltpu.make_async_copy(some, some, r_col.at[it]).wait()
        total = jnp.sum(col_in[it], axis=0)
        cvec[it, mb] = 1.0 / (total * PROTOS)

        def spread(d, carry):
            to = lax.rem(mb + d, NB)
            pltpu.make_async_remote_copy(
                src_ref=cvec.at[it, mb], dst_ref=cvec.at[it, mb],
                send_sem=s_c.at[it], recv_sem=r_c.at[it],
                device_id={"batch": to}, device_id_type=MESH,
            ).start()
            return carry

        lax.fori_loop(1, NB, spread, 0)
        some = cvec.at[it, pl.ds(0, NB - 1)]
        pltpu.make_async_copy(some, some, r_c.at[it]).wait()

    def send_rows(src, dst, k):
        def send(d, carry):
            to = lax.rem(mp + d, NP)
            pltpu.make_async_remote_copy(
                src_ref=src, dst_ref=dst.at[mp],
                send_sem=s_row.at[k], recv_sem=r_row.at[k],
                device_id={"proto": to}, device_id_type=MESH,
            ).start()
            return carry

        lax.fori_loop(1, NP, send, 0)

    def wait_rows(src, dst, k):
        dst[mp] = src[...]
        some = dst.at[pl.ds(0, NP - 1)]
        pltpu.make_async_copy(some, some, r_row.at[k]).wait()
        return jnp.sum(dst[...], axis=0)

    def row_pass(it):
        def step(r, carry):
            rows = pl.ds(pl.multiple_of(r * 64, 64), 64)
            acc = jnp.zeros((64, 128), F32)
            for j in range(64):
                acc = acc + big[rows, pl.ds(j * 128, 128)] * cvec[it, j // 4, pl.ds(j % 4, 1), :]
            part[rows, :] = acc
            return carry

        lax.fori_loop(0, 16, step, 0)

    def col_pass(it):
        for g in range(4):
            def step(i, acc):
                acc = list(acc)
                for u in range(4):
                    rows = pl.ds(pl.multiple_of(i * 32 + u * 8, 8), 8)
                    a = wide[rows, :]
                    for k in range(16):
                        acc[k] = acc[k] + big[rows, pl.ds(g * 2048 + k * 128, 128)] * a
                return tuple(acc)

            acc = lax.fori_loop(0, 32, step, tuple(jnp.zeros((8, 128), F32) for _ in range(16)))
            for k in range(16):
                j = g * 16 + k
                col[it, j // 4, pl.ds(j % 4, 1), :] = jnp.sum(acc[k], axis=0, keepdims=True)

    for it in range(ITERS):
        if it:
            col_pass(it)
        sum_cols(it)
        row_pass(it)
        rvec[it] = rows_to_vec(part)
        send_rows(rvec.at[it], row_in.at[it], it)
        if it == 0:
            def student(r, carry):
                rows = pl.ds(pl.multiple_of(r * 256, 256), 256)
                acc = jnp.zeros((256, 128), F32)
                for j in range(16):
                    s = jnp.dot(us[rows, :], up[:, pl.ds(j * 512, 512)], preferred_element_type=F32)
                    e = jnp.exp2(s * (LOG2E / STUDENT_TEMP))
                    for k in range(4):
                        acc = acc + e[:, k * 128 : (k + 1) * 128]
                part[rows, :] = acc
                return carry

            lax.fori_loop(0, 4, student, 0)
            zvec[...] = rows_to_vec(part)
            send_rows(zvec, z_in, 3)
        total = wait_rows(rvec.at[it], row_in.at[it], it)
        a = 1.0 / (total * CROPS)
        if it < ITERS - 1:
            vec_to_rows(a, wide)

    factor = PROTOS / (STUDENT_TEMP * CROPS)
    z = wait_rows(zvec, z_in, 3)
    vec_to_rows(a * CROPS, wide)
    vec_to_rows(1.0 / z, part)
    xpart = gbuf[1]

    def last(j, carry):
        cols = pl.ds(pl.multiple_of(j * 256, 256), 256)
        w = up[:, cols]
        c0 = cvec[ITERS - 1, j // 2, pl.ds((j % 2) * 2, 1), :]
        c1 = cvec[ITERS - 1, j // 2, pl.ds((j % 2) * 2 + 1, 1), :]
        c = jnp.concatenate([c0, c1], axis=1)
        for i in range(8):
            rows = pl.ds(i * 128, 128)
            s = jnp.dot(us[rows, :], w, preferred_element_type=F32)
            wa = wide[rows, :]
            pz = part[rows, :]
            t = big[rows, cols] * jnp.concatenate([wa, wa], axis=1) * c
            p = jnp.exp2(s * (LOG2E / STUDENT_TEMP)) * jnp.concatenate([pz, pz], axis=1)
            gbuf[0][rows, :] = ((p - t) * factor).astype(BF16)
            ts = t * s
            xpart[rows, :] += ts[:, :128] + ts[:, 128:]
        grad[:, cols] = jnp.dot(ust[...], gbuf[0][...], preferred_element_type=F32)
        return carry

    xpart[...] = jnp.zeros((ROWS, 128), F32)
    lax.fori_loop(0, 32, last, 0)
    xvec[...] = rows_to_vec(xpart) * (1.0 / STUDENT_TEMP)
    send_rows(xvec, x_in, 4)
    x = wait_rows(xvec, x_in, 4)
    loss[...] = jnp.log(z) - x

    for it in range(ITERS):
        some = col.at[it, pl.ds(0, NB - 1)]
        pltpu.make_async_copy(some, some, s_col.at[it]).wait()
        pltpu.make_async_copy(some, some, s_c.at[it]).wait()
    for k in range(5):
        some = z_in.at[pl.ds(0, NP - 1)]
        pltpu.make_async_copy(some, some, s_row.at[k]).wait()


def local(teacher_emb, student_emb, prototypes):
    vmem = pl.BlockSpec(memory_space=pltpu.VMEM)
    loss, grad = pl.pallas_call(
        kernel,
        out_shape=(
            jax.ShapeDtypeStruct((8, 128), F32),
            jax.ShapeDtypeStruct((D, COLS), F32),
        ),
        in_specs=[vmem] * 3,
        out_specs=(vmem, vmem),
        scratch_shapes=[
            pltpu.VMEM((ROWS, D), BF16),
            pltpu.VMEM((ROWS, D), BF16),
            pltpu.VMEM((D, ROWS), BF16),
            pltpu.VMEM((D, COLS), BF16),
            pltpu.VMEM((ROWS, COLS), F32),
            pltpu.VMEM((ROWS, 128), F32),
            pltpu.VMEM((ROWS, 128), F32),
            pltpu.VMEM((ITERS, NB, 4, 128), F32),
            pltpu.VMEM((ITERS, NB, 4, 128), F32),
            pltpu.VMEM((ITERS, NB, 4, 128), F32),
            pltpu.VMEM((ITERS, 8, 128), F32),
            pltpu.VMEM((ITERS, NP, 8, 128), F32),
            [pltpu.VMEM((ROWS, D), BF16), pltpu.VMEM((ROWS, 128), F32)],
            pltpu.VMEM((8, 128), F32),
            pltpu.VMEM((NP, 8, 128), F32),
            pltpu.VMEM((8, 128), F32),
            pltpu.VMEM((NP, 8, 128), F32),
            pltpu.SemaphoreType.DMA((ITERS,)),
            pltpu.SemaphoreType.DMA((ITERS,)),
            pltpu.SemaphoreType.DMA((ITERS,)),
            pltpu.SemaphoreType.DMA((ITERS,)),
            pltpu.SemaphoreType.DMA((5,)),
            pltpu.SemaphoreType.DMA((5,)),
        ],
        compiler_params=pltpu.CompilerParams(
            collective_id=0, has_side_effects=True, vmem_limit_bytes=62 * 1024 * 1024
        ),
    )(teacher_emb, student_emb, prototypes)
    grad = lax.psum_scatter(grad, "batch", scatter_dimension=0, tiled=True)
    return loss.reshape(ROWS), grad


def solution(mesh):
    in_specs = (P("batch", None), P("batch", None), P(None, "proto"))
    out_specs = (P("batch"), P("batch", "proto"))
    return jax.shard_map(local, mesh=mesh, in_specs=in_specs, out_specs=out_specs, check_vma=False)
```

```python
import jax
import jax.numpy as jnp
from jax import lax
from jax.experimental import pallas as pl
from jax.experimental.pallas import tpu as pltpu
from jax.sharding import PartitionSpec as P

PROTOS = 65536
CROPS = 16384
ITERS = 3
TEACHER_TEMP = 0.07
STUDENT_TEMP = 0.1
NP = 8
NX = 4
ROWS = 1024
COLS = 8192
D = 256
MINE = COLS // NX
CH = 512
NQ = MINE // CH
HALF = CH // 2
FACTOR = PROTOS / (STUDENT_TEMP * CROPS)
LOG2E = 1.4426950408889634
MESH = pl.DeviceIdType.MESH
F32 = jnp.float32
BF16 = jnp.bfloat16


def unit(values, axis):
    wide = values.astype(F32)
    return (wide * lax.rsqrt(jnp.sum(wide * wide, axis=axis, keepdims=True) + 1e-06)).astype(BF16)


def rows_to_vec(part):
    out = []
    for i in range(8):
        block = part[pl.ds(i * 128, 128), :]
        out.append(jnp.sum(block.T, axis=0, keepdims=True))
    return jnp.concatenate(out, axis=0)


def vec_to_rows(vec, out):
    for i in range(8):
        out[pl.ds(i * 128, 128), :] = jnp.broadcast_to(vec[i : i + 1, :], (128, 128)).T


def send(src, dst, s, r, **where):
    pltpu.make_async_remote_copy(
        src_ref=src, dst_ref=dst, send_sem=s, recv_sem=r, device_id=where, device_id_type=MESH
    ).start()


def wait(some, sem):
    pltpu.make_async_copy(some, some, sem).wait()


def kernel(
    te, se, pr, loss, grad,
    ut4, us4, ust4, up, big, colv, cin, cb, rvec, row_in, az, az_in,
    land, mine, wa, pz, xp, gb, ring, tot, xv, xv_in,
    s_in, s_col, r_col, s_row, r_row, s_x, r_x, s_z, r_z, s_k, r_k, s_az, r_az,
    s_ring, r_ring, s_out, r_out, s_xv, r_xv,
):
    mb = lax.axis_index("batch")
    mp = lax.axis_index("proto")
    y, x = mb // NX, lax.rem(mb, NX)
    other = mp + 1 - 2 * lax.rem(mp, 2)
    wide, part = wa.at[0], wa.at[1]
    gg = big.at[pl.ds(0, D), pl.ds(0, MINE)]

    def at_x(d):
        return y * NX + lax.rem(x + d, NX)

    def at_y(d):
        return lax.rem(y + d, 4) * NX + x

    def at_z(d):
        return lax.rem(mp + 2 * d, NP)

    barrier = pltpu.get_barrier_semaphore()
    for d in (1, 2, 3):
        pl.semaphore_signal(barrier, inc=1, device_id={"batch": at_x(d)}, device_id_type=MESH)
        pl.semaphore_signal(barrier, inc=1, device_id={"batch": at_y(d)}, device_id_type=MESH)
    for d in range(1, NP):
        pl.semaphore_signal(barrier, inc=1, device_id={"proto": lax.rem(mp + d, NP)}, device_id_type=MESH)

    fetch = [pltpu.make_async_copy(te, ut4.at[0], s_in.at[0]), pltpu.make_async_copy(se, us4.at[0], s_in.at[1])]
    for j in range(4):
        cols = pl.ds(j * 2048, 2048)
        fetch.append(pltpu.make_async_copy(pr.at[:, cols], up.at[:, cols], s_in.at[2 + j]))
    for copy in fetch:
        copy.start()
    fetch[0].wait()
    ut4[0] = unit(ut4[0], 1)
    fetch[1].wait()
    us4[0] = unit(us4[0], 1)
    slab = pl.ds(pl.multiple_of(mp * 128, 128), 128)
    mine[0] = ut4[0, slab, :].astype(F32)
    mine[1] = us4[0, slab, :].astype(F32)
    pl.semaphore_wait(barrier, 6 + NP - 1)

    send(mine, land.at[mp, 2], s_x.at[0], r_x.at[0], batch=at_x(1))
    send(mine, land.at[mp, 0], s_x.at[1], r_x.at[1], batch=at_x(3))

    for j in range(4):
        fetch[2 + j].wait()

    def first(j, carry):
        for k in range(4):
            some = pl.ds(pl.multiple_of(j * 2048 + k * 512, 512), 512)
            up[:, some] = unit(up[:, some], 0)
        cols = pl.ds(pl.multiple_of(j * 2048, 2048), 2048)
        w = up[:, cols]
        total = jnp.zeros((8, 2048), F32)
        for i in range(8):
            rows = pl.ds(i * 128, 128)
            e = jnp.exp2(jnp.dot(ut4[0, rows, :], w, preferred_element_type=F32) * (LOG2E / TEACHER_TEMP))
            big[rows, cols] = e
            total = total + jnp.sum(e.reshape(16, 8, 2048), axis=0)
        flat = jnp.sum(total, axis=0, keepdims=True)
        for k in range(16):
            colv[0, 0, pl.ds(j * 16 + k, 1), :] = flat[:, k * 128 : (k + 1) * 128]
        return carry

    lax.fori_loop(0, 4, first, 0)

    def col_send(it, ph):
        src = colv.at[it, ph]
        for d in (2, 1, 3):
            for h in range(2):
                half = pl.ds(32 * h, 32)
                to = at_y(d) if h == ph else at_x(d)
                send(src.at[half], cin.at[it, ph, d - 1, half], s_col.at[it, ph], r_col.at[it, ph], batch=to)

    def col_recv(it, ph):
        wait(cin.at[it, ph], r_col.at[it, ph])
        colv[it, ph + 1] = colv[it, ph] + cin[it, ph, 0] + cin[it, ph, 1] + cin[it, ph, 2]

    def spread_cols(it):
        c = 1.0 / (colv[it, 2] * PROTOS)
        for j in range(64):
            cb[:, pl.ds(j * 128, 128)] = jnp.broadcast_to(c[j : j + 1, :], (8, 128))

    def row_pass():
        for g in range(4):
            c = [cb[:, pl.ds(g * 2048 + k * 128, 128)] for k in range(16)]

            def step(i, carry):
                for u in range(4):
                    rows = pl.ds(pl.multiple_of(i * 32 + u * 8, 8), 8)
                    acc = [big[rows, pl.ds(g * 2048 + k * 128, 128)] * c[k] for k in range(4)]
                    for k in range(4, 16):
                        acc[k % 4] = acc[k % 4] + big[rows, pl.ds(g * 2048 + k * 128, 128)] * c[k]
                    s = (acc[0] + acc[1]) + (acc[2] + acc[3])
                    part[rows, :] = s if g == 0 else part[rows, :] + s
                return carry

            lax.fori_loop(0, 32, step, 0)

    def col_pass(it):
        for g in range(4):
            def step(i, acc):
                acc = list(acc)
                for u in range(4):
                    rows = pl.ds(pl.multiple_of(i * 32 + u * 8, 8), 8)
                    a = wide[rows, :]
                    for k in range(16):
                        acc[k] = acc[k] + big[rows, pl.ds(g * 2048 + k * 128, 128)] * a
                return tuple(acc)

            acc = lax.fori_loop(0, 32, step, tuple(jnp.zeros((8, 128), F32) for _ in range(16)))
            for k in range(16):
                colv[it, 0, pl.ds(g * 16 + k, 1), :] = jnp.sum(acc[k], axis=0, keepdims=True)

    def row_send(src, dst, k):
        for d in (4, 3, 5, 2, 6, 7, 1):
            send(src, dst.at[mp], s_row.at[k], r_row.at[k], proto=lax.rem(mp + d, NP))

    def row_recv(src, dst, k):
        dst[mp] = src[...]
        wait(dst.at[pl.ds(0, NP - 1)], r_row.at[k])
        return jnp.sum(dst[...], axis=0)

    def student(lo, hi):
        def step(r, carry):
            rows = pl.ds(pl.multiple_of(r * 256, 256), 256)
            acc = jnp.zeros((256, 128), F32)
            for j in range(16):
                s = jnp.dot(us4[0, rows, :], up[:, pl.ds(j * 512, 512)], preferred_element_type=F32)
                e = jnp.exp2(s * (LOG2E / STUDENT_TEMP))
                for k in range(4):
                    acc = acc + e[:, k * 128 : (k + 1) * 128]
            xp[0, rows, :] = acc
            return carry

        lax.fori_loop(lo, hi, step, 0)

    def slabs(p):
        rows = pl.ds(pl.multiple_of(p * 128, 128), 128)
        for d in (1, 2, 3):
            ut4[d, rows, :] = land[p, d - 1, 0].astype(BF16)
            v = land[p, d - 1, 1]
            us4[d, rows, :] = v.astype(BF16)
            ust4[d, :, rows] = v.T.astype(BF16)

    z1, z3, z2 = at_z(1), at_z(3), at_z(2)

    col_send(0, 0)
    student(0, 2)
    col_recv(0, 0)
    col_send(0, 1)
    wait(mine, r_x.at[0])
    wait(mine, r_x.at[1])
    send(land.at[mp, 2, 0], land.at[mp, 1, 0], s_x.at[2], r_x.at[2], batch=at_x(1))
    send(land.at[mp, 0, 1], land.at[mp, 1, 1], s_x.at[3], r_x.at[3], batch=at_x(3))
    student(2, 4)
    rvec[3] = rows_to_vec(xp.at[0])
    col_recv(0, 1)
    spread_cols(0)
    row_pass()
    rvec[0] = rows_to_vec(part)
    row_send(rvec.at[0], row_in.at[0], 0)
    row_send(rvec.at[3], row_in.at[3], 3)
    wait(land.at[mp, 1, 0], r_x.at[2])
    wait(land.at[mp, 1, 1], r_x.at[3])
    send(land.at[mp, :, 0], land.at[mp, :, 0], s_z.at[0], r_z.at[0], proto=z1)
    send(land.at[mp, :, 0], land.at[mp, :, 0], s_z.at[1], r_z.at[1], proto=z3)
    send(land.at[mp, 0, 1], land.at[mp, 0, 1], s_z.at[2], r_z.at[2], proto=z1)
    send(land.at[mp, 0, 1], land.at[mp, 0, 1], s_z.at[3], r_z.at[3], proto=z3)
    send(land.at[mp], land.at[mp], s_k.at[0], r_k.at[0], proto=other)
    for i in range(8):
        block = us4[0, pl.ds(i * 128, 128), :]
        ust4[0, :, pl.ds(i * 128, 128)] = block.astype(F32).T.astype(BF16)
    total = row_recv(rvec.at[0], row_in.at[0], 0)
    vec_to_rows(1.0 / (total * CROPS), wide)

    col_pass(1)
    col_send(1, 0)
    z = row_recv(rvec.at[3], row_in.at[3], 3)
    az[0] = FACTOR / z
    slabs(mp)
    col_recv(1, 0)
    col_send(1, 1)
    col_recv(1, 1)
    spread_cols(1)
    row_pass()
    rvec[1] = rows_to_vec(part)
    row_send(rvec.at[1], row_in.at[1], 1)
    wait(land.at[mp, :, 0], r_z.at[0])
    wait(land.at[mp, :, 0], r_z.at[1])
    wait(land.at[mp, 0, 1], r_z.at[2])
    wait(land.at[mp, 0, 1], r_z.at[3])
    late = pl.ds(1, 2)
    send(land.at[z3, :, 0], land.at[z3, :, 0], s_z.at[4], r_z.at[4], proto=z1)
    send(land.at[mp, late, 1], land.at[mp, late, 1], s_z.at[5], r_z.at[5], proto=z3)
    send(land.at[mp, late, 1], land.at[mp, late, 1], s_z.at[6], r_z.at[6], proto=z1)
    wait(land.at[other], r_k.at[0])
    slabs(other)
    total = row_recv(rvec.at[1], row_in.at[1], 1)
    vec_to_rows(1.0 / (total * CROPS), wide)

    col_pass(2)
    col_send(2, 0)
    col_recv(2, 0)
    col_send(2, 1)
    wait(land.at[mp, late, 1], r_z.at[5])
    wait(land.at[mp, late, 1], r_z.at[6])
    send(land.at[z1, :, 1], land.at[z1, :, 1], s_z.at[7], r_z.at[7], proto=z3)
    send(land.at[z1], land.at[z1], s_k.at[1], r_k.at[1], proto=other)
    send(land.at[z3], land.at[z3], s_k.at[2], r_k.at[2], proto=other)
    slabs(z1)
    slabs(z3)
    col_recv(2, 1)
    spread_cols(2)
    row_pass()
    rvec[2] = rows_to_vec(part)
    row_send(rvec.at[2], row_in.at[2], 2)
    wait(land.at[z2, :, 0], r_z.at[4])
    wait(land.at[z2, :, 1], r_z.at[7])
    send(land.at[z2], land.at[z2], s_k.at[3], r_k.at[3], proto=other)
    slabs(z2)
    total = row_recv(rvec.at[2], row_in.at[2], 2)
    az[1] = FACTOR / total
    for d in (1, 2, 3):
        send(az, az_in.at[3 - d], s_az, r_az, batch=at_x(d))
    vec_to_rows(az[0], pz.at[0])
    vec_to_rows(az[1], wa.at[0])

    base = x * MINE

    def block(q, g):
        cols = pl.ds(pl.multiple_of(base + q * CH, CH), CH)
        w = up[:, cols]
        c = cb[pl.ds(0, 1), cols]
        n = CH // 128
        for b in range(4):
            rows = pl.ds(b * 256, 256)
            s = jnp.dot(us4[g, rows, :], w, preferred_element_type=F32)
            t = jnp.exp2(jnp.dot(ut4[g, rows, :], w, preferred_element_type=F32) * (LOG2E / TEACHER_TEMP))
            t = t * jnp.concatenate([wa[g, rows, :]] * n, axis=1) * c
            p = jnp.exp2(s * (LOG2E / STUDENT_TEMP)) * jnp.concatenate([pz[g, rows, :]] * n, axis=1)
            gb[rows, :] = (p - t).astype(BF16)
            ts = t * s
            ts = (ts[:, :128] + ts[:, 128:256]) + (ts[:, 256:384] + ts[:, 384:])
            xp[g, rows, :] = ts if q == 0 else xp[g, rows, :] + ts
        return jnp.dot(ust4[g], gb[...], preferred_element_type=F32)

    def ring_first(q):
        for h in range(2):
            lanes = pl.ds(q * CH + h * HALF, HALF)
            near, far = (1, 3) if h == 0 else (3, 1)
            opposite = pl.ds(pl.multiple_of(lax.rem(y + 2, 4) * 64, 64), 64)
            direct = pl.ds(pl.multiple_of(lax.rem(y + near, 4) * 64, 64), 64)
            send(gg.at[opposite, lanes], ring.at[q, h, 0], s_ring.at[q, h, 0], r_ring.at[q, h, 0], batch=at_y(far))
            send(gg.at[direct, lanes], ring.at[q, h, 1], s_ring.at[q, h, 1], r_ring.at[q, h, 1], batch=at_y(near))

    def ring_second(q):
        for h in range(2):
            lanes = pl.ds(q * CH + h * HALF, HALF)
            far = 3 if h == 0 else 1
            theirs = pl.ds(pl.multiple_of(lax.rem(y + far, 4) * 64, 64), 64)
            wait(ring.at[q, h, 0], r_ring.at[q, h, 0])
            ring[q, h, 0] = ring[q, h, 0] + gg[theirs, lanes]
            send(ring.at[q, h, 0], ring.at[q, h, 2], s_ring.at[q, h, 2], r_ring.at[q, h, 2], batch=at_y(far))

    def ring_last(q):
        rows = pl.ds(pl.multiple_of(y * 64, 64), 64)
        for h in range(2):
            lanes = pl.ds(q * CH + h * HALF, HALF)
            wait(ring.at[q, h, 1], r_ring.at[q, h, 1])
            wait(ring.at[q, h, 2], r_ring.at[q, h, 2])
            tot[q, :, pl.ds(h * HALF, HALF)] = gg[rows, lanes] + ring[q, h, 1] + ring[q, h, 2]
        cols = pl.ds(pl.multiple_of(base + q * CH, CH), CH)
        for d in (2, 1, 3):
            to = lax.rem(x + d, NX)
            send(tot.at[q, pl.ds(pl.multiple_of(to * 16, 16), 16)], grad.at[:, cols], s_out, r_out, batch=at_x(d))
        grad[:, cols] = tot[q, pl.ds(pl.multiple_of(x * 16, 16), 16)]

    for q in range(NQ):
        lanes = pl.ds(q * CH, CH)
        gg[:, lanes] = block(q, 0)
        if q == 0:
            for k, p in ((1, at_z(1)), (2, at_z(3)), (3, at_z(2))):
                theirs = p + 1 - 2 * lax.rem(p, 2)
                wait(land.at[theirs], r_k.at[k])
                slabs(theirs)
            wait(az_in, r_az)
            for g in (1, 2, 3):
                vec_to_rows(az_in[g - 1, 0], pz.at[g])
                vec_to_rows(az_in[g - 1, 1], wa.at[g])

        def more(g, carry):
            gg[:, lanes] += block(q, g)
            return carry

        lax.fori_loop(1, 4, more, 0)
        ring_first(q)
        if q >= 1:
            ring_second(q - 1)
        if q >= 2:
            ring_last(q - 2)
    for g in range(4):
        xv[g] = rows_to_vec(xp.at[g])
    for d in (1, 2, 3):
        send(xv.at[d], xv_in.at[3 - d], s_xv, r_xv, batch=at_x(d))
    ring_second(NQ - 1)
    ring_last(NQ - 2)
    wait(xv_in, r_xv)
    rvec[4] = (xv[0] + xv_in[0] + xv_in[1] + xv_in[2]) * (1.0 / (FACTOR * STUDENT_TEMP))
    row_send(rvec.at[4], row_in.at[4], 4)
    ring_last(NQ - 1)
    cross = row_recv(rvec.at[4], row_in.at[4], 4)
    loss[...] = jnp.log(z) - cross

    wait(grad.at[:, pl.ds(0, 3 * MINE)], r_out)
    wait(grad.at[:, pl.ds(0, 3 * MINE)], s_out)
    for it in range(ITERS):
        for ph in range(2):
            wait(cin.at[it, ph], s_col.at[it, ph])
    for k in range(5):
        wait(row_in.at[k, pl.ds(0, NP - 1)], s_row.at[k])
    for k in range(2):
        wait(mine, s_x.at[k])
        wait(mine.at[0], s_x.at[2 + k])
    for k, some in (
        (0, land.at[mp, :, 0]), (1, land.at[mp, :, 0]), (2, land.at[mp, 0, 0]), (3, land.at[mp, 0, 0]),
        (4, land.at[mp, :, 0]), (5, land.at[mp, late, 0]), (6, land.at[mp, late, 0]), (7, land.at[mp, :, 0]),
    ):
        wait(some, s_z.at[k])
    for k in range(4):
        wait(land.at[mp], s_k.at[k])
    wait(az_in, s_az)
    wait(xv_in, s_xv)
    for q in range(NQ):
        for h in range(2):
            for k in range(3):
                wait(ring.at[q, h, k], s_ring.at[q, h, k])


def local(teacher_emb, student_emb, prototypes):
    vmem = pl.BlockSpec(memory_space=pltpu.VMEM)
    hbm = pl.BlockSpec(memory_space=pl.ANY)
    dma = pltpu.SemaphoreType.DMA
    loss, grad = pl.pallas_call(
        kernel,
        out_shape=(
            jax.ShapeDtypeStruct((8, 128), F32),
            jax.ShapeDtypeStruct((16, COLS), F32),
        ),
        in_specs=[hbm] * 3,
        out_specs=(vmem, vmem),
        scratch_shapes=[
            pltpu.VMEM((NX, ROWS, D), BF16),
            pltpu.VMEM((NX, ROWS, D), BF16),
            pltpu.VMEM((NX, D, ROWS), BF16),
            pltpu.VMEM((D, COLS), BF16),
            pltpu.VMEM((ROWS, COLS), F32),
            pltpu.VMEM((ITERS, 3, 64, 128), F32),
            pltpu.VMEM((ITERS, 2, 3, 64, 128), F32),
            pltpu.VMEM((8, COLS), F32),
            pltpu.VMEM((5, 8, 128), F32),
            pltpu.VMEM((5, NP, 8, 128), F32),
            pltpu.VMEM((2, 8, 128), F32),
            pltpu.VMEM((3, 2, 8, 128), F32),
            pltpu.VMEM((NP, 3, 2, 128, D), F32),
            pltpu.VMEM((2, 128, D), F32),
            pltpu.VMEM((NX, ROWS, 128), F32),
            pltpu.VMEM((NX, ROWS, 128), F32),
            pltpu.VMEM((NX, ROWS, 128), F32),
            pltpu.VMEM((ROWS, CH), BF16),
            pltpu.VMEM((NQ, 2, 3, 64, HALF), F32),
            pltpu.VMEM((NQ, 64, CH), F32),
            pltpu.VMEM((NX, 8, 128), F32),
            pltpu.VMEM((3, 8, 128), F32),
            dma((6,)),
            dma((ITERS, 2)), dma((ITERS, 2)),
            dma((5,)), dma((5,)),
            dma((4,)), dma((4,)),
            dma((8,)), dma((8,)),
            dma((4,)), dma((4,)),
            dma, dma,
            dma((NQ, 2, 3)), dma((NQ, 2, 3)),
            dma, dma,
            dma, dma,
        ],
        compiler_params=pltpu.CompilerParams(
            collective_id=0, has_side_effects=True, vmem_limit_bytes=63 * 1024 * 1024
        ),
    )(teacher_emb, student_emb, prototypes)
    return loss.reshape(ROWS), grad


def solution(mesh):
    in_specs = (P("batch", None), P("batch", None), P(None, "proto"))
    out_specs = (P("batch"), P("batch", "proto"))
    return jax.shard_map(local, mesh=mesh, in_specs=in_specs, out_specs=out_specs, check_vma=False)
```

```python
import jax
import jax.numpy as jnp
from jax import lax
from jax.experimental import pallas as pl
from jax.experimental.pallas import tpu as pltpu
from jax.sharding import PartitionSpec as P

PROTOS = 65536
CROPS = 16384
ITERS = 3
TEACHER_TEMP = 0.07
STUDENT_TEMP = 0.1
NP = 8
NX = 4
ROWS = 1024
COLS = 8192
D = 256
MINE = COLS // NX
CH = 512
NQ = MINE // CH
HALF = CH // 2
FACTOR = PROTOS / (STUDENT_TEMP * CROPS)
LOG2E = 1.4426950408889634
MESH = pl.DeviceIdType.MESH
F32 = jnp.float32
BF16 = jnp.bfloat16


def unit(values, axis):
    wide = values.astype(F32)
    return (wide * lax.rsqrt(jnp.sum(wide * wide, axis=axis, keepdims=True) + 1e-06)).astype(BF16)


def rows_to_vec(part):
    out = []
    for i in range(8):
        block = part[pl.ds(i * 128, 128), :]
        out.append(jnp.sum(block.T, axis=0, keepdims=True))
    return jnp.concatenate(out, axis=0)


def vec_to_rows(vec, out):
    for i in range(8):
        out[pl.ds(i * 128, 128), :] = jnp.broadcast_to(vec[i : i + 1, :], (128, 128)).T


def send(src, dst, s, r, **where):
    pltpu.make_async_remote_copy(
        src_ref=src, dst_ref=dst, send_sem=s, recv_sem=r, device_id=where, device_id_type=MESH
    ).start()


def wait(some, sem):
    pltpu.make_async_copy(some, some, sem).wait()


def kernel(
    te, se, pr, loss, grad,
    ut, us, ust, up, big, colv, cin, cb, rvec, row_in, az, az_in,
    land, mine, pz, gb, ring,
    s_in, s_col, r_col, s_row, r_row, s_x, r_x, s_z, r_z, s_k, r_k, s_az, r_az,
    s_ring, r_ring, s_out, r_out,
):
    mb = lax.axis_index("batch")
    mp = lax.axis_index("proto")
    y, x = mb // NX, lax.rem(mb, NX)
    other = mp + 1 - 2 * lax.rem(mp, 2)
    gg = big.at[pl.ds(0, D), pl.ds(0, MINE)]
    wa = [big.at[:, pl.ds(MINE + 128 * d, 128)] for d in range(4)]
    ut0, us0 = gb.at[pl.ds(0, ROWS), pl.ds(0, D)], gb.at[pl.ds(ROWS, ROWS), pl.ds(0, D)]
    wide, part, xp = pz.at[1], pz.at[2], pz.at[3]

    def at_x(d):
        return y * NX + lax.rem(x + d, NX)

    def at_y(d):
        return lax.rem(y + d, 4) * NX + x

    def at_z(d):
        return lax.rem(mp + 2 * d, NP)

    barrier = pltpu.get_barrier_semaphore()
    for d in (1, 2, 3):
        pl.semaphore_signal(barrier, inc=1, device_id={"batch": at_x(d)}, device_id_type=MESH)
        pl.semaphore_signal(barrier, inc=1, device_id={"batch": at_y(d)}, device_id_type=MESH)
    for d in range(1, NP):
        pl.semaphore_signal(barrier, inc=1, device_id={"proto": lax.rem(mp + d, NP)}, device_id_type=MESH)

    fetch = [pltpu.make_async_copy(te, ut0, s_in.at[0]), pltpu.make_async_copy(se, us0, s_in.at[1])]
    for j in range(4):
        cols = pl.ds(j * 2048, 2048)
        fetch.append(pltpu.make_async_copy(pr.at[:, cols], up.at[:, cols], s_in.at[2 + j]))
    for copy in fetch:
        copy.start()
    fetch[0].wait()
    ut0[...] = unit(ut0[...], 1)
    fetch[1].wait()
    us0[...] = unit(us0[...], 1)
    slab = pl.ds(pl.multiple_of(mp * 128, 128), 128)
    mine[0, 0] = ut0[slab, :].astype(F32)
    mine[0, 1] = us0[slab, :].astype(F32)
    pl.semaphore_wait(barrier, 6 + NP - 1)

    def x_near(i, p):
        send(mine.at[i], land.at[p, 2], s_x.at[i, 0], r_x.at[i, 0], batch=at_x(1))
        send(mine.at[i], land.at[p, 0], s_x.at[i, 1], r_x.at[i, 1], batch=at_x(3))

    def x_far(i, p):
        wait(mine.at[0], r_x.at[i, 0])
        wait(mine.at[0], r_x.at[i, 1])
        send(land.at[p, 2, 0], land.at[p, 1, 0], s_x.at[i, 2], r_x.at[i, 2], batch=at_x(1))
        send(land.at[p, 0, 1], land.at[p, 1, 1], s_x.at[i, 3], r_x.at[i, 3], batch=at_x(3))

    def x_done(i, p):
        wait(land.at[p, 1, 0], r_x.at[i, 2])
        wait(land.at[p, 1, 1], r_x.at[i, 3])

    x_near(0, mp)

    def col_send(it, ph, k):
        on_x = lax.rem(k + ph, 2)
        on_y = 1 - on_x
        for d in (2, 1, 3):
            to = lax.rem(y + d * on_y, 4) * NX + lax.rem(x + d * on_x, NX)
            send(colv.at[it, ph, k], cin.at[it, ph, k, d - 1], s_col.at[it, ph, k], r_col.at[it, ph, k], batch=to)

    def col_recv(it, ph, k):
        wait(cin.at[it, ph, k], r_col.at[it, ph, k])
        colv[it, ph + 1, k] = colv[it, ph, k] + cin[it, ph, k, 0] + cin[it, ph, k, 1] + cin[it, ph, k, 2]

    def first(j, carry):
        cols = pl.ds(pl.multiple_of(j * 2048, 2048), 2048)
        pltpu.make_async_copy(pr.at[:, cols], up.at[:, cols], s_in.at[2 + j]).wait()
        for k in range(4):
            some = pl.ds(pl.multiple_of(j * 2048 + k * 512, 512), 512)
            up[:, some] = unit(up[:, some], 0)
        w = up[:, cols]
        total = jnp.zeros((8, 2048), F32)
        for i in range(8):
            rows = pl.ds(i * 128, 128)
            e = jnp.exp2(jnp.dot(ut0[rows, :], w, preferred_element_type=F32) * (LOG2E / TEACHER_TEMP))
            big[rows, cols] = e
            total = total + jnp.sum(e.reshape(16, 8, 2048), axis=0)
        flat = jnp.sum(total, axis=0, keepdims=True)
        for k in range(16):
            colv[0, 0, j, pl.ds(k, 1), :] = flat[:, k * 128 : (k + 1) * 128]
        col_send(0, 0, j)
        return carry

    lax.fori_loop(0, 4, first, 0)

    def row_pass(it, g):
        v = 1.0 / (colv[it, 2, g] * PROTOS)
        for j in range(16):
            cb[:, pl.ds((g * 16 + j) * 128, 128)] = jnp.broadcast_to(v[j : j + 1, :], (8, 128))
        c = [cb[:, pl.ds((g * 16 + k) * 128, 128)] for k in range(16)]

        def step(i, carry):
            res = []
            for u in range(16):
                rows = pl.ds(pl.multiple_of(i * 128, 128) + u * 8, 8)
                acc = [big[rows, pl.ds(g * 2048 + k * 128, 128)] * c[k] for k in range(4)]
                for k in range(4, 16):
                    acc[k % 4] = acc[k % 4] + big[rows, pl.ds(g * 2048 + k * 128, 128)] * c[k]
                total = (acc[0] + acc[1]) + (acc[2] + acc[3])
                res.append(total if g == 0 else part[rows, :] + total)
            for u in range(16):
                part[pl.ds(pl.multiple_of(i * 128, 128) + u * 8, 8), :] = res[u]
            return carry

        lax.fori_loop(0, 8, step, 0)

    def col_pass(it):
        for g in range(4):
            def step(i, acc):
                acc = list(acc)
                for u in range(4):
                    rows = pl.ds(pl.multiple_of(i * 32, 32) + u * 8, 8)
                    a = wide[rows, :]
                    for k in range(16):
                        acc[k] = acc[k] + big[rows, pl.ds(g * 2048 + k * 128, 128)] * a
                return tuple(acc)

            acc = lax.fori_loop(0, 32, step, tuple(jnp.zeros((8, 128), F32) for _ in range(16)))
            for k in range(16):
                colv[it, 0, g, pl.ds(k, 1), :] = jnp.sum(acc[k], axis=0, keepdims=True)
            col_send(it, 0, g)

    def row_send(src, dst, k):
        for d in (4, 3, 5, 2, 6, 7, 1):
            send(src, dst.at[mp], s_row.at[k], r_row.at[k], proto=lax.rem(mp + d, NP))

    def row_recv(src, dst, k):
        dst[mp] = src[...]
        wait(dst.at[pl.ds(0, NP - 1)], r_row.at[k])
        return jnp.sum(dst[...], axis=0)

    def student(r):
        rows = pl.ds(r * 256, 256)
        acc = jnp.zeros((256, 128), F32)
        for j in range(16):
            s = jnp.dot(us0[rows, :], up[:, pl.ds(j * 512, 512)], preferred_element_type=F32)
            e = jnp.exp2(s * (LOG2E / STUDENT_TEMP))
            for k in range(4):
                acc = acc + e[:, k * 128 : (k + 1) * 128]
        xp[rows, :] = acc

    def cross(lo, hi):
        def step(r, carry):
            rows = pl.ds(pl.multiple_of(r * 256, 256), 256)
            v = jnp.zeros((256, D), F32)
            for g in range(4):
                cols = pl.ds(g * 2048, 2048)
                kc = (big[rows, cols] * cb[pl.ds(0, 1), cols]).astype(BF16)
                v = v + lax.dot_general(kc, up[:, cols], (((1,), (1,)), ((), ())), preferred_element_type=F32)
            v = v * us0[rows, :].astype(F32)
            part[rows, :] = v[:, :128] + v[:, 128:]
            return carry

        lax.fori_loop(lo, hi, step, 0)

    def slabs(p):
        for d in (1, 2, 3):
            rows = pl.ds(pl.multiple_of(p * 512, 512) + d * 128, 128)
            cols = pl.ds(pl.multiple_of(p * 512 + d * 128, 128), 128)
            ut[rows, :] = land[p, d - 1, 0].astype(BF16)
            v = land[p, d - 1, 1]
            us[rows, :] = v.astype(BF16)
            ust[:, cols] = v.T.astype(BF16)

    z1, z3, z2 = at_z(1), at_z(3), at_z(2)

    col_recv(0, 0, 0)
    col_send(0, 1, 0)
    student(0)
    col_recv(0, 0, 1)
    col_send(0, 1, 1)
    col_recv(0, 0, 2)
    col_send(0, 1, 2)
    student(1)
    col_recv(0, 0, 3)
    col_send(0, 1, 3)
    x_far(0, mp)
    for k in range(4):
        col_recv(0, 1, k)
        row_pass(0, k)
    rvec[0] = rows_to_vec(part)
    row_send(rvec.at[0], row_in.at[0], 0)
    x_done(0, mp)
    most = pl.ds(0, 2)
    for k, to in ((0, z1), (1, z3)):
        send(land.at[mp, :, 0], land.at[mp, :, 0], s_z.at[0, k], r_z.at[0, k], proto=to)
    for k, to in ((0, z1), (1, z3)):
        send(land.at[mp, most, 1], land.at[mp, most, 1], s_z.at[1, k], r_z.at[1, k], proto=to)
    send(land.at[mp], land.at[mp], s_k.at[0], r_k.at[0], proto=other)
    slab = pl.ds(pl.multiple_of(z2 * 128, 128), 128)
    mine[1, 0] = ut0[slab, :].astype(F32)
    mine[1, 1] = us0[slab, :].astype(F32)
    x_near(1, z2)
    student(2)
    student(3)
    rvec[3] = rows_to_vec(xp)
    total = row_recv(rvec.at[0], row_in.at[0], 0)
    vec_to_rows(1.0 / (total * CROPS), wide)

    col_pass(1)
    for i in range(8):
        v = us0[pl.ds(i * 128, 128), :]
        us[pl.ds(i * 512, 128), :] = v
        ust[:, pl.ds(i * 512, 128)] = v.astype(F32).T.astype(BF16)
        ut[pl.ds(i * 512, 128), :] = ut0[pl.ds(i * 128, 128), :]
    slabs(mp)
    for k in range(4):
        col_recv(1, 0, k)
        col_send(1, 1, k)
    for k in range(4):
        col_recv(1, 1, k)
        row_pass(1, k)
    rvec[1] = rows_to_vec(part)
    row_send(rvec.at[1], row_in.at[1], 1)
    row_send(rvec.at[3], row_in.at[3], 3)
    for k, to in ((0, z1), (1, z3)):
        send(land.at[mp, 2, 1], land.at[mp, 2, 1], s_z.at[2, k], r_z.at[2, k], proto=to)
    x_far(1, z2)
    wait(land.at[other], r_k.at[0])
    slabs(other)
    total = row_recv(rvec.at[1], row_in.at[1], 1)
    vec_to_rows(1.0 / (total * CROPS), wide)

    col_pass(2)
    z = row_recv(rvec.at[3], row_in.at[3], 3)
    az[0] = FACTOR / z
    for d in (1, 2, 3):
        send(az.at[0], az_in.at[0, 3 - d], s_az.at[0], r_az.at[0], batch=at_x(d))
    for k in range(2):
        wait(land.at[mp, :, 0], r_z.at[0, k])
        wait(land.at[mp, most, 1], r_z.at[1, k])
        wait(land.at[mp, 2, 1], r_z.at[2, k])
    x_done(1, z2)
    for k, p in ((1, z1), (2, z3), (3, z2)):
        send(land.at[p], land.at[p], s_k.at[k], r_k.at[k], proto=other)
    for k in range(4):
        col_recv(2, 0, k)
        col_send(2, 1, k)
    wait(az_in.at[0], r_az.at[0])
    vec_to_rows(az[0], pz.at[0])
    vec_to_rows(az_in[0, 0], pz.at[1])
    vec_to_rows(az_in[0, 2], pz.at[3])
    for k in range(4):
        col_recv(2, 1, k)
        row_pass(2, k)
    rvec[2] = rows_to_vec(part)
    row_send(rvec.at[2], row_in.at[2], 2)
    slabs(z1)
    slabs(z3)
    slabs(z2)
    for k, p in ((1, z1), (2, z3), (3, z2)):
        theirs = p + 1 - 2 * lax.rem(p, 2)
        wait(land.at[theirs], r_k.at[k])
        slabs(theirs)
    cross(0, 2)
    total = row_recv(rvec.at[2], row_in.at[2], 2)
    az[1] = FACTOR / total
    for d in (1, 2, 3):
        send(az.at[1], az_in.at[1, 3 - d], s_az.at[1], r_az.at[1], batch=at_x(d))
    cross(2, 4)
    rvec[4] = rows_to_vec(part) / (total * STUDENT_TEMP)
    row_send(rvec.at[4], row_in.at[4], 4)
    vec_to_rows(az[1], wa[0])
    vec_to_rows(az_in[0, 1], pz.at[2])
    wait(az_in.at[1], r_az.at[1])
    for g in (1, 2, 3):
        vec_to_rows(az_in[1, g - 1], wa[g])

    base = x * MINE

    def block(q):
        cols = pl.ds(pl.multiple_of(base + q * CH, CH), CH)
        w = up[:, cols]
        c = cb[pl.ds(0, 1), cols]
        n = CH // 128
        for p in range(8):
            rows = pl.ds(p * 512, 512)
            own = pl.ds(p * 128, 128)
            s = jnp.dot(us[rows, :], w, preferred_element_type=F32)
            t = jnp.dot(ut[rows, :], w, preferred_element_type=F32)
            a = jnp.concatenate([wa[d][own, :] for d in range(4)], axis=0)
            e = jnp.concatenate([pz[d, own, :] for d in range(4)], axis=0)
            t = jnp.exp2(t * (LOG2E / TEACHER_TEMP)) * jnp.concatenate([a] * n, axis=1) * c
            s = jnp.exp2(s * (LOG2E / STUDENT_TEMP)) * jnp.concatenate([e] * n, axis=1)
            gb[rows, :] = (s - t).astype(BF16)
        gg[:, pl.ds(pl.multiple_of(q * CH, CH), CH)] = jnp.dot(ust[...], gb[...], preferred_element_type=F32)

    def lanes_of(q, h):
        return pl.ds(pl.multiple_of(q * CH + h * HALF, HALF), HALF)

    def rows_of(d):
        return pl.ds(pl.multiple_of(lax.rem(y + d, 4) * 64, 64), 64)

    def ring_first(q):
        for h in range(2):
            near, far = (1, 3) if h == 0 else (3, 1)
            send(gg.at[rows_of(2), lanes_of(q, h)], ring.at[q, h, 0], s_ring.at[q, h, 0], r_ring.at[q, h, 0], batch=at_y(far))
            send(gg.at[rows_of(near), lanes_of(q, h)], ring.at[q, h, 1], s_ring.at[q, h, 1], r_ring.at[q, h, 1], batch=at_y(near))

    def ring_second(q):
        for h in range(2):
            far = 3 if h == 0 else 1
            wait(ring.at[q, h, 0], r_ring.at[q, h, 0])
            ring[q, h, 0] = ring[q, h, 0] + gg[rows_of(far), lanes_of(q, h)]
            send(ring.at[q, h, 0], ring.at[q, h, 2], s_ring.at[q, h, 2], r_ring.at[q, h, 2], batch=at_y(far))

    def ring_last(q):
        for h in range(2):
            wait(ring.at[q, h, 1], r_ring.at[q, h, 1])
            wait(ring.at[q, h, 2], r_ring.at[q, h, 2])
            ring[q, h, 1] = gg[rows_of(0), lanes_of(q, h)] + ring[q, h, 1] + ring[q, h, 2]
            cols = pl.ds(pl.multiple_of(base + q * CH + h * HALF, HALF), HALF)
            for d in (2, 1, 3):
                to = pl.ds(pl.multiple_of(lax.rem(x + d, NX) * 16, 16), 16)
                send(ring.at[q, h, 1, to], grad.at[:, cols], s_out, r_out, batch=at_x(d))
            grad[:, cols] = ring[q, h, 1, pl.ds(pl.multiple_of(x * 16, 16), 16)]

    def last(q, carry):
        @pl.when(q < NQ)
        def _():
            block(q)
            ring_first(q)

        @pl.when((q >= 1) & (q <= NQ))
        def _():
            ring_second(q - 1)

        @pl.when(q >= 2)
        def _():
            ring_last(q - 2)

        return carry

    lax.fori_loop(0, NQ + 2, last, 0)
    loss[...] = jnp.log(z) - row_recv(rvec.at[4], row_in.at[4], 4)

    wait(grad.at[:, pl.ds(0, 3 * MINE)], r_out)
    wait(grad.at[:, pl.ds(0, 3 * MINE)], s_out)
    for it in range(ITERS):
        for ph in range(2):
            for k in range(4):
                wait(cin.at[it, ph, k], s_col.at[it, ph, k])
    for k in range(5):
        wait(row_in.at[k, pl.ds(0, NP - 1)], s_row.at[k])
    for i in range(2):
        for k in range(2):
            wait(mine.at[0], s_x.at[i, k])
            wait(mine.at[0, 0], s_x.at[i, 2 + k])
    for k in range(2):
        wait(land.at[mp, :, 0], s_z.at[0, k])
        wait(land.at[mp, most, 1], s_z.at[1, k])
        wait(land.at[mp, 2, 1], s_z.at[2, k])
    for k in range(4):
        wait(land.at[mp], s_k.at[k])
    for k in range(2):
        wait(az_in.at[k], s_az.at[k])
    for q in range(NQ):
        for h in range(2):
            for k in range(3):
                wait(ring.at[q, h, k], s_ring.at[q, h, k])


def handover(loss, grad, loss_out, grad_out):
    loss_out[...] = loss[...]
    grad_out[...] = grad[...]


def local(teacher_emb, student_emb, prototypes):
    vmem = pl.BlockSpec(memory_space=pltpu.VMEM)
    hbm = pl.BlockSpec(memory_space=pl.ANY)
    dma = pltpu.SemaphoreType.DMA
    loss, grad = pl.pallas_call(
        kernel,
        out_shape=(
            jax.ShapeDtypeStruct((8, 128), F32),
            jax.ShapeDtypeStruct((16, COLS), F32),
        ),
        in_specs=[hbm] * 3,
        out_specs=(vmem, vmem),
        scratch_shapes=[
            pltpu.VMEM((NX * ROWS, D), BF16),
            pltpu.VMEM((NX * ROWS, D), BF16),
            pltpu.VMEM((D, NX * ROWS), BF16),
            pltpu.VMEM((D, COLS), BF16),
            pltpu.VMEM((ROWS, COLS), F32),
            pltpu.VMEM((ITERS, 3, 4, 16, 128), F32),
            pltpu.VMEM((ITERS, 2, 4, 3, 16, 128), F32),
            pltpu.VMEM((8, COLS), F32),
            pltpu.VMEM((5, 8, 128), F32),
            pltpu.VMEM((5, NP, 8, 128), F32),
            pltpu.VMEM((2, 8, 128), F32),
            pltpu.VMEM((2, 3, 8, 128), F32),
            pltpu.VMEM((NP, 3, 2, 128, D), F32),
            pltpu.VMEM((2, 2, 128, D), F32),
            pltpu.VMEM((NX, ROWS, 128), F32),
            pltpu.VMEM((NX * ROWS, CH), BF16),
            pltpu.VMEM((NQ, 2, 3, 64, HALF), F32),
            dma((6,)),
            dma((ITERS, 2, 4)), dma((ITERS, 2, 4)),
            dma((5,)), dma((5,)),
            dma((2, 4)), dma((2, 4)),
            dma((3, 2)), dma((3, 2)),
            dma((4,)), dma((4,)),
            dma((2,)), dma((2,)),
            dma((NQ, 2, 3)), dma((NQ, 2, 3)),
            dma, dma,
        ],
        compiler_params=pltpu.CompilerParams(
            collective_id=0, has_side_effects=True, vmem_limit_bytes=63 * 1024 * 1024
        ),
    )(teacher_emb, student_emb, prototypes)
    loss, grad = pl.pallas_call(
        handover,
        out_shape=(
            jax.ShapeDtypeStruct((8, 128), F32),
            jax.ShapeDtypeStruct((16, COLS), F32),
        ),
        in_specs=[vmem] * 2,
        out_specs=(vmem, vmem),
    )(loss, grad)
    return loss.reshape(ROWS), grad


def solution(mesh):
    in_specs = (P("batch", None), P("batch", None), P(None, "proto"))
    out_specs = (P("batch"), P("batch", "proto"))
    return jax.shard_map(local, mesh=mesh, in_specs=in_specs, out_specs=out_specs, check_vma=False)
```

```python
import jax
import jax.numpy as jnp
from jax import lax
from jax.experimental import pallas as pl
from jax.experimental.pallas import tpu as pltpu
from jax.sharding import PartitionSpec as P

PROTOS = 65536
CROPS = 16384
ITERS = 3
TEACHER_TEMP = 0.07
STUDENT_TEMP = 0.1
NP = 8
NX = 4
ROWS = 1024
COLS = 8192
D = 256
MINE = COLS // NX
CH = 256
NQ = MINE // CH
LAG = 4
FACTOR = PROTOS / (STUDENT_TEMP * CROPS)
CROSS = 1.0 / STUDENT_TEMP
LOG2E = 1.4426950408889634
MESH = pl.DeviceIdType.MESH
F32 = jnp.float32
BF16 = jnp.bfloat16


def unit(values, axis):
    wide = values.astype(F32)
    return (wide * lax.rsqrt(jnp.sum(wide * wide, axis=axis, keepdims=True) + 1e-06)).astype(BF16)


def rows_to_vec(part):
    out = []
    for i in range(8):
        block = part[pl.ds(i * 128, 128), :]
        out.append(jnp.sum(block.T, axis=0, keepdims=True))
    return jnp.concatenate(out, axis=0)


def vec_to_rows(vec, out):
    for i in range(8):
        out[pl.ds(i * 128, 128), :] = jnp.broadcast_to(vec[i : i + 1, :], (128, 128)).T


def send(src, dst, s, r, **where):
    pltpu.make_async_remote_copy(
        src_ref=src, dst_ref=dst, send_sem=s, recv_sem=r, device_id=where, device_id_type=MESH
    ).start()


def wait(some, sem):
    pltpu.make_async_copy(some, some, sem).wait()


def kernel(
    te, se, pr, loss, grad,
    ut, us, ust, up, big, colv, cin, cb, rvec, row_in, az, az_in, row_all,
    land, mine, pz, gb, ring, tot,
    s_in, s_col, r_col, s_row, r_row, s_x, r_x, s_z, r_z, s_k, r_k, s_az, r_az, s_all, r_all,
    s_ring, r_ring, s_out, r_out, s_own,
):
    mb = lax.axis_index("batch")
    mp = lax.axis_index("proto")
    y, x = mb // NX, lax.rem(mb, NX)
    other = mp + 1 - 2 * lax.rem(mp, 2)
    ut0, us0 = gb.at[pl.ds(0, ROWS), pl.ds(0, D)], gb.at[pl.ds(ROWS, ROWS), pl.ds(0, D)]
    wide, part, xp = pz.at[1], pz.at[2], pz.at[3]

    def at_x(d):
        return y * NX + lax.rem(x + d, NX)

    def at_y(d):
        return lax.rem(y + d, 4) * NX + x

    def at_z(d):
        return lax.rem(mp + 2 * d, NP)

    fetch = [pltpu.make_async_copy(te, ut0, s_in.at[0]), pltpu.make_async_copy(se, us0, s_in.at[1])]
    for j in range(4):
        cols = pl.ds(j * 2048, 2048)
        fetch.append(pltpu.make_async_copy(pr.at[:, cols], up.at[:, cols], s_in.at[2 + j]))
    for copy in fetch:
        copy.start()
    barrier = pltpu.get_barrier_semaphore()
    for d in (1, 2, 3):
        pl.semaphore_signal(barrier, inc=1, device_id={"batch": at_y(d)}, device_id_type=MESH)

    def greet(i, carry):
        there = {"batch": at_x(i // NP), "proto": lax.rem(mp + i, NP)}
        pl.semaphore_signal(barrier, inc=1, device_id=there, device_id_type=MESH)
        return carry

    lax.fori_loop(1, NX * NP, greet, 0)

    fetch[0].wait()
    ut0[...] = unit(ut0[...], 1)
    fetch[1].wait()
    us0[...] = unit(us0[...], 1)
    slab = pl.ds(pl.multiple_of(mp * 128, 128), 128)
    mine[0, 0] = ut0[slab, :].astype(F32)
    mine[0, 1] = us0[slab, :].astype(F32)
    def x_near(i, p):
        send(mine.at[i], land.at[p, 2], s_x.at[i, 0], r_x.at[i, 0], batch=at_x(1))
        send(mine.at[i], land.at[p, 0], s_x.at[i, 1], r_x.at[i, 1], batch=at_x(3))

    def x_far(i, p):
        wait(mine.at[0], r_x.at[i, 0])
        wait(mine.at[0], r_x.at[i, 1])
        send(land.at[p, 2, 0], land.at[p, 1, 0], s_x.at[i, 2], r_x.at[i, 2], batch=at_x(1))
        send(land.at[p, 0, 1], land.at[p, 1, 1], s_x.at[i, 3], r_x.at[i, 3], batch=at_x(3))

    def x_done(i, p):
        wait(land.at[p, 1, 0], r_x.at[i, 2])
        wait(land.at[p, 1, 1], r_x.at[i, 3])


    def col_send(it, ph, k):
        for d in (2, 1, 3):
            to = at_x(d) if ph else at_y(d)
            send(colv.at[it, ph, k], cin.at[it, ph, k, d - 1], s_col.at[it, ph, k], r_col.at[it, ph, k], batch=to)

    def col_recv(it, ph, k):
        wait(cin.at[it, ph, k], r_col.at[it, ph, k])
        colv[it, ph + 1, k] = colv[it, ph, k] + cin[it, ph, k, 0] + cin[it, ph, k, 1] + cin[it, ph, k, 2]

    def first(j, carry):
        cols = pl.ds(pl.multiple_of(j * 2048, 2048), 2048)
        pltpu.make_async_copy(pr.at[:, cols], up.at[:, cols], s_in.at[2 + j]).wait()
        for k in range(4):
            some = pl.ds(pl.multiple_of(j * 2048 + k * 512, 512), 512)
            up[:, some] = unit(up[:, some], 0)
        w = up[:, cols]
        total = jnp.zeros((8, 2048), F32)
        for i in range(8):
            rows = pl.ds(i * 128, 128)
            e = jnp.exp2(jnp.dot(ut0[rows, :], w, preferred_element_type=F32) * (LOG2E / TEACHER_TEMP))
            big[rows, cols] = e
            total = total + jnp.sum(e.reshape(16, 8, 2048), axis=0)
        flat = jnp.sum(total, axis=0, keepdims=True)
        for k in range(16):
            colv[0, 0, j, pl.ds(k, 1), :] = flat[:, k * 128 : (k + 1) * 128]
        @pl.when(j == 0)
        def _():
            pl.semaphore_wait(barrier, 3 + NX * NP - 1)
            x_near(0, mp)

        col_send(0, 0, j)
        return carry

    lax.fori_loop(0, 4, first, 0)

    def row_pass(it, g):
        v = 1.0 / (colv[it, 2, g] * PROTOS)
        for j in range(16):
            cb[:, pl.ds((g * 16 + j) * 128, 128)] = jnp.broadcast_to(v[j : j + 1, :], (8, 128))
        c = [cb[:, pl.ds((g * 16 + k) * 128, 128)] for k in range(16)]

        def step(i, carry):
            res = []
            for u in range(16):
                rows = pl.ds(pl.multiple_of(i * 128, 128) + u * 8, 8)
                acc = [big[rows, pl.ds(g * 2048 + k * 128, 128)] * c[k] for k in range(4)]
                for k in range(4, 16):
                    acc[k % 4] = acc[k % 4] + big[rows, pl.ds(g * 2048 + k * 128, 128)] * c[k]
                total = (acc[0] + acc[1]) + (acc[2] + acc[3])
                res.append(total if g == 0 else part[rows, :] + total)
            for u in range(16):
                part[pl.ds(pl.multiple_of(i * 128, 128) + u * 8, 8), :] = res[u]
            return carry

        lax.fori_loop(0, 8, step, 0)

    def col_pass(it):
        for g in range(4):
            def step(i, acc):
                acc = list(acc)
                for u in range(4):
                    rows = pl.ds(pl.multiple_of(i * 32, 32) + u * 8, 8)
                    a = wide[rows, :]
                    for k in range(16):
                        acc[k] = acc[k] + big[rows, pl.ds(g * 2048 + k * 128, 128)] * a
                return tuple(acc)

            acc = lax.fori_loop(0, 32, step, tuple(jnp.zeros((8, 128), F32) for _ in range(16)))
            for k in range(16):
                colv[it, 0, g, pl.ds(k, 1), :] = jnp.sum(acc[k], axis=0, keepdims=True)
            col_send(it, 0, g)

    def row_send(src, dst, k):
        for d in (4, 3, 5, 2, 6, 7, 1):
            send(src, dst.at[mp], s_row.at[k], r_row.at[k], proto=lax.rem(mp + d, NP))

    def row_recv(src, dst, k):
        dst[mp] = src[...]
        wait(dst.at[pl.ds(0, NP - 1)], r_row.at[k])
        return jnp.sum(dst[...], axis=0)

    def student(lo, hi):
        def step(r, carry):
            rows = pl.ds(pl.multiple_of(r * 256, 256), 256)
            acc = jnp.zeros((256, 128), F32)
            for j in range(16):
                s = jnp.dot(us0[rows, :], up[:, pl.ds(j * 512, 512)], preferred_element_type=F32)
                e = jnp.exp2(s * (LOG2E / STUDENT_TEMP))
                for k in range(4):
                    acc = acc + e[:, k * 128 : (k + 1) * 128]
            xp[rows, :] = acc
            return carry

        lax.fori_loop(lo, hi, step, 0)

    def cross(r):
        rows = pl.ds(pl.multiple_of(r * 256, 256), 256)
        v = jnp.zeros((256, D), F32)
        for g in range(4):
            cols = pl.ds(g * 2048, 2048)
            kc = (big[rows, cols] * cb[pl.ds(0, 1), cols]).astype(BF16)
            v = v + lax.dot_general(kc, up[:, cols], (((1,), (1,)), ((), ())), preferred_element_type=F32)
        v = v * mine_us(r)
        v = v[:, :128] + v[:, 128:]
        for i in range(2):
            rvec[4, pl.ds(2 * r + i, 1), :] = jnp.sum(v[i * 128 : (i + 1) * 128].T, axis=0, keepdims=True)

    def mine_us(r):
        own = [us[pl.ds(pl.multiple_of((2 * r + i) * 512, 512), 128), :] for i in range(2)]
        return jnp.concatenate(own, axis=0).astype(F32)

    def slabs(p):
        for d in (1, 2, 3):
            rows = pl.ds(pl.multiple_of(p * 512, 512) + d * 128, 128)
            cols = pl.ds(pl.multiple_of(p * 512 + d * 128, 128), 128)
            ut[rows, :] = land[p, d - 1, 0].astype(BF16)
            v = land[p, d - 1, 1]
            us[rows, :] = v.astype(BF16)
            ust[:, cols] = v.T.astype(BF16)

    z1, z3, z2 = at_z(1), at_z(3), at_z(2)

    for k in range(2):
        col_recv(0, 0, k)
        col_send(0, 1, k)
    student(0, 2)
    for k in (2, 3):
        col_recv(0, 0, k)
        col_send(0, 1, k)
    x_far(0, mp)
    for k in range(4):
        col_recv(0, 1, k)
        row_pass(0, k)
    rvec[0] = rows_to_vec(part)
    row_send(rvec.at[0], row_in.at[0], 0)
    x_done(0, mp)
    most = pl.ds(0, 2)
    for k, to in ((0, z1), (1, z3)):
        send(land.at[mp, :, 0], land.at[mp, :, 0], s_z.at[0, k], r_z.at[0, k], proto=to)
    for k, to in ((0, z1), (1, z3)):
        send(land.at[mp, most, 1], land.at[mp, most, 1], s_z.at[1, k], r_z.at[1, k], proto=to)
    send(land.at[mp], land.at[mp], s_k.at[0], r_k.at[0], proto=other)
    slab = pl.ds(pl.multiple_of(z2 * 128, 128), 128)
    mine[1, 0] = ut0[slab, :].astype(F32)
    mine[1, 1] = us0[slab, :].astype(F32)
    x_near(1, z2)
    student(2, 4)
    rvec[3] = rows_to_vec(xp)
    total = row_recv(rvec.at[0], row_in.at[0], 0)
    vec_to_rows(1.0 / (total * CROPS), wide)

    col_pass(1)
    for i in range(8):
        v = us0[pl.ds(i * 128, 128), :]
        us[pl.ds(i * 512, 128), :] = v
        ust[:, pl.ds(i * 512, 128)] = v.astype(F32).T.astype(BF16)
        ut[pl.ds(i * 512, 128), :] = ut0[pl.ds(i * 128, 128), :]
    slabs(mp)
    for k in range(4):
        col_recv(1, 0, k)
        col_send(1, 1, k)
    for k in range(4):
        col_recv(1, 1, k)
        row_pass(1, k)
    rvec[1] = rows_to_vec(part)
    row_send(rvec.at[1], row_in.at[1], 1)
    row_send(rvec.at[3], row_in.at[3], 3)
    for k, to in ((0, z1), (1, z3)):
        send(land.at[mp, 2, 1], land.at[mp, 2, 1], s_z.at[2, k], r_z.at[2, k], proto=to)
    x_far(1, z2)
    wait(land.at[other], r_k.at[0])
    slabs(other)
    total = row_recv(rvec.at[1], row_in.at[1], 1)
    vec_to_rows(1.0 / (total * CROPS), wide)

    col_pass(2)
    z = row_recv(rvec.at[3], row_in.at[3], 3)
    az[...] = FACTOR / z
    for d in (1, 2, 3):
        send(az, az_in.at[0, 3 - d], s_az, r_az, batch=at_x(d))
    for k in range(2):
        wait(land.at[mp, :, 0], r_z.at[0, k])
        wait(land.at[mp, most, 1], r_z.at[1, k])
        wait(land.at[mp, 2, 1], r_z.at[2, k])
    x_done(1, z2)
    for k, p in ((1, z1), (2, z3), (3, z2)):
        send(land.at[p], land.at[p], s_k.at[k], r_k.at[k], proto=other)
    for k in range(4):
        col_recv(2, 0, k)
        col_send(2, 1, k)
    wait(az_in.at[0, pl.ds(0, 3)], r_az)
    vec_to_rows(az[...], pz.at[0])
    vec_to_rows(az_in[0, 0], pz.at[1])
    vec_to_rows(az_in[0, 2], pz.at[3])
    for k in range(4):
        col_recv(2, 1, k)
        row_pass(2, k)
    rvec[2] = rows_to_vec(part)

    def to_all(i, carry):
        e = i // NP
        there = lax.rem(mp + i, NP)
        pltpu.make_async_remote_copy(
            src_ref=rvec.at[2], dst_ref=row_all.at[lax.rem(NX - e, NX) * NP + mp], send_sem=s_all, recv_sem=r_all,
            device_id={"batch": at_x(e), "proto": there}, device_id_type=MESH,
        ).start()
        return carry

    lax.fori_loop(1, NX * NP, to_all, 0)
    row_all[mp] = rvec[2]
    slabs(z1)
    slabs(z3)
    slabs(z2)
    for k, p in ((1, z1), (2, z3), (3, z2)):
        theirs = p + 1 - 2 * lax.rem(p, 2)
        wait(land.at[theirs], r_k.at[k])
        slabs(theirs)
    vec_to_rows(az_in[0, 1], pz.at[2])
    for k in range(4):
        wait(land.at[mp], s_k.at[k])
    for k in range(2):
        wait(land.at[mp, :, 0], s_z.at[0, k])
        wait(land.at[mp, most, 1], s_z.at[1, k])
        wait(land.at[mp, 2, 1], s_z.at[2, k])
        for i in range(2):
            wait(mine.at[0, 0], s_x.at[i, 2 + k])
    wait(row_all.at[pl.ds(0, NX * NP - 1)], r_all)
    for d in range(NX):
        az_in[1, d] = FACTOR / jnp.sum(row_all[pl.ds(d * NP, NP)], axis=0)

    base = x * MINE

    def block(q):
        cols = pl.ds(pl.multiple_of(base + q * CH, CH), CH)
        w = up[:, cols]
        c = cb[pl.ds(0, 1), cols]
        n = CH // 128
        for p in range(8):
            rows = pl.ds(p * 512, 512)
            own = pl.ds(p * 128, 128)
            s = jnp.dot(us[rows, :], w, preferred_element_type=F32)
            t = jnp.dot(ut[rows, :], w, preferred_element_type=F32)
            a = [jnp.broadcast_to(az_in[1, d, p : p + 1, :], (128, 128)).T for d in range(4)]
            a = jnp.concatenate(a, axis=0)
            e = jnp.concatenate([pz[d, own, :] for d in range(4)], axis=0)
            t = jnp.exp2(t * (LOG2E / TEACHER_TEMP)) * jnp.concatenate([a] * n, axis=1) * c
            s = jnp.exp2(s * (LOG2E / STUDENT_TEMP)) * jnp.concatenate([e] * n, axis=1)
            gb[rows, :] = (s - t).astype(BF16)
        g = jnp.dot(ust[...], gb[...], preferred_element_type=F32)
        land[q, 0, 0] = g[:128]
        land[q, 0, 1] = g[128:]

    def part_of(q, h, d):
        to = lax.rem(y + d, 4)
        return land.at[q, 0, to // 2, pl.ds(pl.multiple_of(lax.rem(to, 2) * 64 + h * 32, 32), 32)]

    def ring_first(q):
        for h in range(2):
            near, far = (1, 3) if h == 0 else (3, 1)
            send(part_of(q, h, 2), ring.at[q, h, 0], s_ring.at[q, h, 0], r_ring.at[q, h, 0], batch=at_y(far))
            send(part_of(q, h, near), ring.at[q, h, 1], s_ring.at[q, h, 1], r_ring.at[q, h, 1], batch=at_y(near))

    def ring_second(q):
        for h in range(2):
            far = 3 if h == 0 else 1
            wait(ring.at[q, h, 0], r_ring.at[q, h, 0])
            ring[q, h, 0] = ring[q, h, 0] + part_of(q, h, far)[...]
            send(ring.at[q, h, 0], ring.at[q, h, 2], s_ring.at[q, h, 2], r_ring.at[q, h, 2], batch=at_y(far))

    def ring_last(q):
        for h in range(2):
            wait(ring.at[q, h, 1], r_ring.at[q, h, 1])
            wait(ring.at[q, h, 2], r_ring.at[q, h, 2])
            tot[q, pl.ds(h * 32, 32)] = part_of(q, h, 0)[...] + ring[q, h, 1] + ring[q, h, 2]
        cols = pl.ds(pl.multiple_of(base + q * CH, CH), CH)
        for d in (2, 1, 3):
            to = pl.ds(pl.multiple_of(lax.rem(x + d, NX) * 16, 16), 16)
            send(tot.at[q, to], grad.at[:, cols], s_out, r_out, batch=at_x(d))
        pltpu.make_async_copy(tot.at[q, pl.ds(pl.multiple_of(x * 16, 16), 16)], grad.at[:, cols], s_own).start()

    def last(q, carry):
        @pl.when(q < NQ)
        def _():
            block(q)
            ring_first(q)

        @pl.when((q >= LAG) & (q < NQ + LAG))
        def _():
            ring_second(q - LAG)

        @pl.when(q >= 2 * LAG)
        def _():
            ring_last(q - 2 * LAG)

        @pl.when((q >= NQ) & (q < NQ + 4))
        def _():
            cross(q - NQ)

        @pl.when(q == NQ + 3)
        def _():
            rvec[4] = rvec[4] * CROSS / jnp.sum(row_all[pl.ds(0, NP)], axis=0)
            row_send(rvec.at[4], row_in.at[4], 4)

        return carry

    lax.fori_loop(0, NQ + 2 * LAG, last, 0)
    loss[...] = jnp.log(z) - row_recv(rvec.at[4], row_in.at[4], 4)

    wait(grad.at[:, pl.ds(0, 3 * MINE)], r_out)
    wait(grad.at[:, pl.ds(0, 3 * MINE)], s_out)
    wait(grad.at[:, pl.ds(0, MINE)], s_own)
    for it in range(ITERS):
        for ph in range(2):
            for k in range(4):
                wait(cin.at[it, ph, k], s_col.at[it, ph, k])
    for k in (0, 1, 3, 4):
        wait(row_in.at[k, pl.ds(0, NP - 1)], s_row.at[k])
    for i in range(2):
        for k in range(2):
            wait(mine.at[0], s_x.at[i, k])
    wait(az_in.at[0, pl.ds(0, 3)], s_az)
    wait(row_all.at[pl.ds(0, NX * NP - 1)], s_all)
    for q in range(NQ):
        for h in range(2):
            for k in range(3):
                wait(ring.at[q, h, k], s_ring.at[q, h, k])


def handover(loss, grad, loss_out, grad_out):
    loss_out[...] = loss[...]
    grad_out[...] = grad[...]


def local(teacher_emb, student_emb, prototypes):
    vmem = pl.BlockSpec(memory_space=pltpu.VMEM)
    hbm = pl.BlockSpec(memory_space=pl.ANY)
    dma = pltpu.SemaphoreType.DMA
    loss, grad = pl.pallas_call(
        kernel,
        out_shape=(
            jax.ShapeDtypeStruct((8, 128), F32),
            jax.ShapeDtypeStruct((16, COLS), F32),
        ),
        in_specs=[hbm] * 3,
        out_specs=(vmem, hbm),
        scratch_shapes=[
            pltpu.VMEM((NX * ROWS, D), BF16),
            pltpu.VMEM((NX * ROWS, D), BF16),
            pltpu.VMEM((D, NX * ROWS), BF16),
            pltpu.VMEM((D, COLS), BF16),
            pltpu.VMEM((ROWS, COLS), F32),
            pltpu.VMEM((ITERS, 3, 4, 16, 128), F32),
            pltpu.VMEM((ITERS, 2, 4, 3, 16, 128), F32),
            pltpu.VMEM((8, COLS), F32),
            pltpu.VMEM((5, 8, 128), F32),
            pltpu.VMEM((5, NP, 8, 128), F32),
            pltpu.VMEM((8, 128), F32),
            pltpu.VMEM((2, NX, 8, 128), F32),
            pltpu.VMEM((NX * NP, 8, 128), F32),
            pltpu.VMEM((NP, 3, 2, 128, D), F32),
            pltpu.VMEM((2, 2, 128, D), F32),
            pltpu.VMEM((NX, ROWS, 128), F32),
            pltpu.VMEM((NX * ROWS, CH), BF16),
            pltpu.VMEM((NQ, 2, 3, 32, CH), F32),
            pltpu.VMEM((NQ, 64, CH), F32),
            dma((6,)),
            dma((ITERS, 2, 4)), dma((ITERS, 2, 4)),
            dma((5,)), dma((5,)),
            dma((2, 4)), dma((2, 4)),
            dma((3, 2)), dma((3, 2)),
            dma((4,)), dma((4,)),
            dma, dma,
            dma, dma,
            dma((NQ, 2, 3)), dma((NQ, 2, 3)),
            dma, dma, dma,
        ],
        compiler_params=pltpu.CompilerParams(
            collective_id=0, has_side_effects=True, vmem_limit_bytes=63 * 1024 * 1024
        ),
    )(teacher_emb, student_emb, prototypes)
    loss, grad = pl.pallas_call(
        handover,
        out_shape=(
            jax.ShapeDtypeStruct((8, 128), F32),
            jax.ShapeDtypeStruct((16, COLS), F32),
        ),
        in_specs=[vmem] * 2,
        out_specs=(vmem, vmem),
    )(loss, grad)
    return loss.reshape(ROWS), grad


def solution(mesh):
    in_specs = (P("batch", None), P("batch", None), P(None, "proto"))
    out_specs = (P("batch"), P("batch", "proto"))
    return jax.shard_map(local, mesh=mesh, in_specs=in_specs, out_specs=out_specs, check_vma=False)
```

```python
import jax
import jax.numpy as jnp
from jax import lax
from jax.experimental import pallas as pl
from jax.experimental.pallas import tpu as pltpu
from jax.sharding import PartitionSpec as P

PROTOS = 65536
CROPS = 16384
ITERS = 3
TEACHER_TEMP = 0.07
STUDENT_TEMP = 0.1
NP = 8
NX = 4
ROWS = 1024
COLS = 8192
D = 256
MINE = COLS // NX
CH = 256
NQ = MINE // CH
LAG = 4
FACTOR = PROTOS / (STUDENT_TEMP * CROPS)
CROSS = 1.0 / STUDENT_TEMP
LOG2E = 1.4426950408889634
MESH = pl.DeviceIdType.MESH
F32 = jnp.float32
BF16 = jnp.bfloat16


def unit(values, axis):
    wide = values.astype(F32)
    return (wide * lax.rsqrt(jnp.sum(wide * wide, axis=axis, keepdims=True) + 1e-06)).astype(BF16)


def rows_to_vec(part):
    out = []
    for i in range(8):
        block = part[pl.ds(i * 128, 128), :]
        out.append(jnp.sum(block.T, axis=0, keepdims=True))
    return jnp.concatenate(out, axis=0)


def vec_to_rows(vec, out):
    for i in range(8):
        out[pl.ds(i * 128, 128), :] = jnp.broadcast_to(vec[i : i + 1, :], (128, 128)).T


def send(src, dst, s, r, **where):
    pltpu.make_async_remote_copy(
        src_ref=src, dst_ref=dst, send_sem=s, recv_sem=r, device_id=where, device_id_type=MESH
    ).start()


def wait(some, sem):
    pltpu.make_async_copy(some, some, sem).wait()


def kernel(
    te, se, pr, loss, grad,
    ut, us, ust, up, big, colv, cin, cb, rvec, row_in, az, az_in, row_all,
    land, mine, pz, gb, ring, tot,
    s_in, s_col, r_col, s_row, r_row, s_x, r_x, s_z, r_z, s_k, r_k, s_az, r_az, s_all, r_all,
    s_ring, r_ring, s_out, r_out, s_own,
):
    mb = lax.axis_index("batch")
    mp = lax.axis_index("proto")
    y, x = mb // NX, lax.rem(mb, NX)
    other = mp + 1 - 2 * lax.rem(mp, 2)
    ut0, us0 = gb.at[pl.ds(0, ROWS), pl.ds(0, D)], gb.at[pl.ds(ROWS, ROWS), pl.ds(0, D)]
    wide, part, xp = pz.at[1], pz.at[2], pz.at[3]

    def at_x(d):
        return y * NX + lax.rem(x + d, NX)

    def at_y(d):
        return lax.rem(y + d, 4) * NX + x

    def at_z(d):
        return lax.rem(mp + 2 * d, NP)

    fetch = [pltpu.make_async_copy(te, ut0, s_in.at[0]), pltpu.make_async_copy(se, us0, s_in.at[1])]
    for j in range(4):
        cols = pl.ds(j * 2048, 2048)
        fetch.append(pltpu.make_async_copy(pr.at[:, cols], up.at[:, cols], s_in.at[2 + j]))
    for copy in fetch:
        copy.start()
    barrier = pltpu.get_barrier_semaphore()
    for d in (1, 2, 3):
        pl.semaphore_signal(barrier, inc=1, device_id={"batch": at_y(d)}, device_id_type=MESH)

    def greet(i, carry):
        there = {"batch": at_x(i // NP), "proto": lax.rem(mp + i, NP)}
        pl.semaphore_signal(barrier, inc=1, device_id=there, device_id_type=MESH)
        return carry

    lax.fori_loop(1, NX * NP, greet, 0)

    fetch[0].wait()
    ut0[...] = unit(ut0[...], 1)
    fetch[1].wait()
    us0[...] = unit(us0[...], 1)
    slab = pl.ds(pl.multiple_of(mp * 128, 128), 128)
    mine[0, 0] = ut0[slab, :].astype(F32)
    mine[0, 1] = us0[slab, :].astype(F32)
    def x_near(i, p):
        send(mine.at[i], land.at[p, 2], s_x.at[i, 0], r_x.at[i, 0], batch=at_x(1))
        send(mine.at[i], land.at[p, 0], s_x.at[i, 1], r_x.at[i, 1], batch=at_x(3))

    def x_far(i, p):
        wait(mine.at[0], r_x.at[i, 0])
        wait(mine.at[0], r_x.at[i, 1])
        send(land.at[p, 2, 0], land.at[p, 1, 0], s_x.at[i, 2], r_x.at[i, 2], batch=at_x(1))
        send(land.at[p, 0, 1], land.at[p, 1, 1], s_x.at[i, 3], r_x.at[i, 3], batch=at_x(3))

    def x_done(i, p):
        wait(land.at[p, 1, 0], r_x.at[i, 2])
        wait(land.at[p, 1, 1], r_x.at[i, 3])


    def col_send(it, ph, k):
        for d in (2, 1, 3):
            to = at_x(d) if ph else at_y(d)
            send(colv.at[it, ph, k], cin.at[it, ph, k, d - 1], s_col, r_col.at[it, ph, k], batch=to)

    def col_recv(it, ph, k):
        wait(cin.at[it, ph, k], r_col.at[it, ph, k])
        colv[it, ph + 1, k] = colv[it, ph, k] + cin[it, ph, k, 0] + cin[it, ph, k, 1] + cin[it, ph, k, 2]

    def first(j, carry):
        cols = pl.ds(pl.multiple_of(j * 2048, 2048), 2048)
        pltpu.make_async_copy(pr.at[:, cols], up.at[:, cols], s_in.at[2 + j]).wait()
        for k in range(4):
            some = pl.ds(pl.multiple_of(j * 2048 + k * 512, 512), 512)
            up[:, some] = unit(up[:, some], 0)
        w = up[:, cols]
        total = jnp.zeros((8, 2048), F32)
        for i in range(8):
            rows = pl.ds(i * 128, 128)
            e = jnp.exp2(jnp.dot(ut0[rows, :], w, preferred_element_type=F32) * (LOG2E / TEACHER_TEMP))
            big[rows, cols] = e
            total = total + jnp.sum(e.reshape(16, 8, 2048), axis=0)
        flat = jnp.sum(total, axis=0, keepdims=True)
        for k in range(16):
            colv[0, 0, j, pl.ds(k, 1), :] = flat[:, k * 128 : (k + 1) * 128]
        @pl.when(j == 0)
        def _():
            pl.semaphore_wait(barrier, 3 + NX * NP - 1)
            x_near(0, mp)

        col_send(0, 0, j)
        return carry

    lax.fori_loop(0, 4, first, 0)

    def row_pass(it, g):
        v = 1.0 / (colv[it, 2, g] * PROTOS)
        for j in range(16):
            cb[:, pl.ds((g * 16 + j) * 128, 128)] = jnp.broadcast_to(v[j : j + 1, :], (8, 128))
        c = [cb[:, pl.ds((g * 16 + k) * 128, 128)] for k in range(16)]

        def step(i, carry):
            res = []
            for u in range(16):
                rows = pl.ds(pl.multiple_of(i * 128, 128) + u * 8, 8)
                acc = [big[rows, pl.ds(g * 2048 + k * 128, 128)] * c[k] for k in range(4)]
                for k in range(4, 16):
                    acc[k % 4] = acc[k % 4] + big[rows, pl.ds(g * 2048 + k * 128, 128)] * c[k]
                total = (acc[0] + acc[1]) + (acc[2] + acc[3])
                res.append(total if g == 0 else part[rows, :] + total)
            for u in range(16):
                part[pl.ds(pl.multiple_of(i * 128, 128) + u * 8, 8), :] = res[u]
            return carry

        lax.fori_loop(0, 8, step, 0)

    def col_pass(it):
        for g in range(4):
            def step(i, acc):
                acc = list(acc)
                for u in range(4):
                    rows = pl.ds(pl.multiple_of(i * 32, 32) + u * 8, 8)
                    a = wide[rows, :]
                    for k in range(16):
                        acc[k] = acc[k] + big[rows, pl.ds(g * 2048 + k * 128, 128)] * a
                return tuple(acc)

            acc = lax.fori_loop(0, 32, step, tuple(jnp.zeros((8, 128), F32) for _ in range(16)))
            for k in range(16):
                colv[it, 0, g, pl.ds(k, 1), :] = jnp.sum(acc[k], axis=0, keepdims=True)
            col_send(it, 0, g)

    def row_send(src, dst, k):
        for d in (4, 3, 5, 2, 6, 7, 1):
            send(src, dst.at[mp], s_row.at[k], r_row.at[k], proto=lax.rem(mp + d, NP))

    def row_recv(src, dst, k):
        dst[mp] = src[...]
        wait(dst.at[pl.ds(0, NP - 1)], r_row.at[k])
        return jnp.sum(dst[...], axis=0)

    def student(lo, hi):
        def step(r, carry):
            rows = pl.ds(pl.multiple_of(r * 256, 256), 256)
            acc = jnp.zeros((256, 128), F32)
            for j in range(16):
                s = jnp.dot(us0[rows, :], up[:, pl.ds(j * 512, 512)], preferred_element_type=F32)
                e = jnp.exp2(s * (LOG2E / STUDENT_TEMP))
                for k in range(4):
                    acc = acc + e[:, k * 128 : (k + 1) * 128]
            xp[rows, :] = acc
            return carry

        lax.fori_loop(lo, hi, step, 0)

    def cross(r):
        rows = pl.ds(pl.multiple_of(r * 256, 256), 256)
        v = jnp.zeros((256, D), F32)
        for g in range(4):
            cols = pl.ds(g * 2048, 2048)
            kc = (big[rows, cols] * cb[pl.ds(0, 1), cols]).astype(BF16)
            v = v + lax.dot_general(kc, up[:, cols], (((1,), (1,)), ((), ())), preferred_element_type=F32)
        v = v * mine_us(r)
        v = v[:, :128] + v[:, 128:]
        for i in range(2):
            rvec[4, pl.ds(2 * r + i, 1), :] = jnp.sum(v[i * 128 : (i + 1) * 128].T, axis=0, keepdims=True)

    def mine_us(r):
        own = [us[pl.ds(pl.multiple_of((2 * r + i) * 512, 512), 128), :] for i in range(2)]
        return jnp.concatenate(own, axis=0).astype(F32)

    def slabs(p):
        for d in (1, 2, 3):
            rows = pl.ds(pl.multiple_of(p * 512, 512) + d * 128, 128)
            cols = pl.ds(pl.multiple_of(p * 512 + d * 128, 128), 128)
            ut[rows, :] = land[p, d - 1, 0].astype(BF16)
            v = land[p, d - 1, 1]
            us[rows, :] = v.astype(BF16)
            ust[:, cols] = v.T.astype(BF16)

    z1, z3, z2 = at_z(1), at_z(3), at_z(2)

    for k in range(2):
        col_recv(0, 0, k)
        col_send(0, 1, k)
    student(0, 2)
    for k in (2, 3):
        col_recv(0, 0, k)
        col_send(0, 1, k)
    x_far(0, mp)
    for k in range(4):
        col_recv(0, 1, k)
        row_pass(0, k)
    rvec[0] = rows_to_vec(part)
    row_send(rvec.at[0], row_in.at[0], 0)
    x_done(0, mp)
    most = pl.ds(0, 2)
    for k, to in ((0, z1), (1, z3)):
        send(land.at[mp, :, 0], land.at[mp, :, 0], s_z.at[0, k], r_z.at[0, k], proto=to)
    for k, to in ((0, z1), (1, z3)):
        send(land.at[mp, most, 1], land.at[mp, most, 1], s_z.at[1, k], r_z.at[1, k], proto=to)
    send(land.at[mp], land.at[mp], s_k.at[0], r_k.at[0], proto=other)
    slab = pl.ds(pl.multiple_of(z2 * 128, 128), 128)
    mine[1, 0] = ut0[slab, :].astype(F32)
    mine[1, 1] = us0[slab, :].astype(F32)
    x_near(1, z2)
    student(2, 4)
    rvec[3] = rows_to_vec(xp)
    total = row_recv(rvec.at[0], row_in.at[0], 0)
    vec_to_rows(1.0 / (total * CROPS), wide)

    col_pass(1)
    for i in range(8):
        v = us0[pl.ds(i * 128, 128), :]
        us[pl.ds(i * 512, 128), :] = v
        ust[:, pl.ds(i * 512, 128)] = v.astype(F32).T.astype(BF16)
        ut[pl.ds(i * 512, 128), :] = ut0[pl.ds(i * 128, 128), :]
    slabs(mp)
    for k in range(4):
        col_recv(1, 0, k)
        col_send(1, 1, k)
    for k in range(4):
        col_recv(1, 1, k)
        row_pass(1, k)
    rvec[1] = rows_to_vec(part)
    row_send(rvec.at[1], row_in.at[1], 1)
    row_send(rvec.at[3], row_in.at[3], 3)
    for k, to in ((0, z1), (1, z3)):
        send(land.at[mp, 2, 1], land.at[mp, 2, 1], s_z.at[2, k], r_z.at[2, k], proto=to)
    x_far(1, z2)
    wait(land.at[other], r_k.at[0])
    slabs(other)
    total = row_recv(rvec.at[1], row_in.at[1], 1)
    vec_to_rows(1.0 / (total * CROPS), wide)

    col_pass(2)
    z = row_recv(rvec.at[3], row_in.at[3], 3)
    az[...] = FACTOR / z
    for d in (1, 2, 3):
        send(az, az_in.at[0, 3 - d], s_az, r_az, batch=at_x(d))
    for k in range(2):
        wait(land.at[mp, :, 0], r_z.at[0, k])
        wait(land.at[mp, most, 1], r_z.at[1, k])
        wait(land.at[mp, 2, 1], r_z.at[2, k])
    x_done(1, z2)
    for k, p in ((1, z1), (2, z3), (3, z2)):
        send(land.at[p], land.at[p], s_k.at[k], r_k.at[k], proto=other)
    for k in range(4):
        col_recv(2, 0, k)
        col_send(2, 1, k)
    wait(az_in.at[0, pl.ds(0, 3)], r_az)
    vec_to_rows(az[...], pz.at[0])
    vec_to_rows(az_in[0, 0], pz.at[1])
    vec_to_rows(az_in[0, 2], pz.at[3])
    for k in range(4):
        col_recv(2, 1, k)
        row_pass(2, k)
    rvec[2] = rows_to_vec(part)

    def to_all(i, carry):
        e = i // NP
        there = lax.rem(mp + i, NP)
        pltpu.make_async_remote_copy(
            src_ref=rvec.at[2], dst_ref=row_all.at[lax.rem(NX - e, NX) * NP + mp], send_sem=s_all, recv_sem=r_all,
            device_id={"batch": at_x(e), "proto": there}, device_id_type=MESH,
        ).start()
        return carry

    lax.fori_loop(1, NX * NP, to_all, 0)
    row_all[mp] = rvec[2]
    slabs(z1)
    slabs(z3)
    slabs(z2)
    for k, p in ((1, z1), (2, z3), (3, z2)):
        theirs = p + 1 - 2 * lax.rem(p, 2)
        wait(land.at[theirs], r_k.at[k])
        slabs(theirs)
    vec_to_rows(az_in[0, 1], pz.at[2])

    def early(r, carry):
        cross(r)
        return carry

    lax.fori_loop(0, 2, early, 0)
    for k in range(4):
        wait(land.at[mp], s_k.at[k])
    for k in range(2):
        wait(land.at[mp, :, 0], s_z.at[0, k])
        wait(land.at[mp, most, 1], s_z.at[1, k])
        wait(land.at[mp, 2, 1], s_z.at[2, k])
        for i in range(2):
            wait(mine.at[0, 0], s_x.at[i, 2 + k])
    wait(row_all.at[pl.ds(0, NX * NP - 1)], r_all)
    for d in range(NX):
        az_in[1, d] = FACTOR / jnp.sum(row_all[pl.ds(d * NP, NP)], axis=0)

    base = x * MINE

    def block(q):
        cols = pl.ds(pl.multiple_of(base + q * CH, CH), CH)
        w = up[:, cols]
        c = cb[pl.ds(0, 1), cols]
        n = CH // 128
        for p in range(8):
            rows = pl.ds(p * 512, 512)
            own = pl.ds(p * 128, 128)
            s = jnp.dot(us[rows, :], w, preferred_element_type=F32)
            t = jnp.dot(ut[rows, :], w, preferred_element_type=F32)
            a = [jnp.broadcast_to(az_in[1, d, p : p + 1, :], (128, 128)).T for d in range(4)]
            a = jnp.concatenate(a, axis=0)
            e = jnp.concatenate([pz[d, own, :] for d in range(4)], axis=0)
            t = jnp.exp2(t * (LOG2E / TEACHER_TEMP)) * jnp.concatenate([a] * n, axis=1) * c
            s = jnp.exp2(s * (LOG2E / STUDENT_TEMP)) * jnp.concatenate([e] * n, axis=1)
            gb[rows, :] = (s - t).astype(BF16)
        g = jnp.dot(ust[...], gb[...], preferred_element_type=F32)
        land[q, 0, 0] = g[:128]
        land[q, 0, 1] = g[128:]

    def part_of(q, h, d):
        to = lax.rem(y + d, 4)
        return land.at[q, 0, to // 2, pl.ds(pl.multiple_of(lax.rem(to, 2) * 64 + h * 32, 32), 32)]

    def ring_first(q):
        for h in range(2):
            near, far = (1, 3) if h == 0 else (3, 1)
            send(part_of(q, h, 2), ring.at[q, h, 0], s_ring, r_ring.at[q, h, 0], batch=at_y(far))
            send(part_of(q, h, near), ring.at[q, h, 1], s_ring, r_ring.at[q, h, 1], batch=at_y(near))

    def ring_second(q):
        for h in range(2):
            far = 3 if h == 0 else 1
            wait(ring.at[q, h, 0], r_ring.at[q, h, 0])
            ring[q, h, 0] = ring[q, h, 0] + part_of(q, h, far)[...]
            send(ring.at[q, h, 0], ring.at[q, h, 2], s_ring, r_ring.at[q, h, 2], batch=at_y(far))

    def ring_last(q):
        for h in range(2):
            wait(ring.at[q, h, 1], r_ring.at[q, h, 1])
            wait(ring.at[q, h, 2], r_ring.at[q, h, 2])
            tot[q, pl.ds(h * 32, 32)] = part_of(q, h, 0)[...] + ring[q, h, 1] + ring[q, h, 2]
        cols = pl.ds(pl.multiple_of(base + q * CH, CH), CH)
        for d in (2, 1, 3):
            to = pl.ds(pl.multiple_of(lax.rem(x + d, NX) * 16, 16), 16)
            send(tot.at[q, to], grad.at[:, cols], s_out, r_out, batch=at_x(d))
        pltpu.make_async_copy(tot.at[q, pl.ds(pl.multiple_of(x * 16, 16), 16)], grad.at[:, cols], s_own).start()

    def last(q, carry):
        @pl.when(q < NQ)
        def _():
            block(q)
            ring_first(q)

        @pl.when((q >= LAG) & (q < NQ + LAG))
        def _():
            ring_second(q - LAG)

        @pl.when(q >= 2 * LAG)
        def _():
            ring_last(q - 2 * LAG)

        @pl.when((q >= NQ) & (q < NQ + 2))
        def _():
            cross(q - NQ + 2)

        @pl.when(q == NQ + 1)
        def _():
            rvec[4] = rvec[4] * CROSS / jnp.sum(row_all[pl.ds(0, NP)], axis=0)
            row_send(rvec.at[4], row_in.at[4], 4)

        return carry

    lax.fori_loop(0, NQ + 2 * LAG, last, 0)
    loss[...] = jnp.log(z) - row_recv(rvec.at[4], row_in.at[4], 4)

    wait(grad.at[:, pl.ds(0, 3 * MINE)], r_out)
    wait(grad.at[:, pl.ds(0, 3 * MINE)], s_out)
    wait(grad.at[:, pl.ds(0, MINE)], s_own)
    wait(cin, s_col)
    for k in (0, 1, 3, 4):
        wait(row_in.at[k, pl.ds(0, NP - 1)], s_row.at[k])
    for i in range(2):
        for k in range(2):
            wait(mine.at[0], s_x.at[i, k])
    wait(az_in.at[0, pl.ds(0, 3)], s_az)
    wait(row_all.at[pl.ds(0, NX * NP - 1)], s_all)
    wait(ring, s_ring)


def handover(loss, grad, loss_out, grad_out):
    loss_out[...] = loss[...]
    grad_out[...] = grad[...]


def local(teacher_emb, student_emb, prototypes):
    vmem = pl.BlockSpec(memory_space=pltpu.VMEM)
    hbm = pl.BlockSpec(memory_space=pl.ANY)
    dma = pltpu.SemaphoreType.DMA
    loss, grad = pl.pallas_call(
        kernel,
        out_shape=(
            jax.ShapeDtypeStruct((8, 128), F32),
            jax.ShapeDtypeStruct((16, COLS), F32),
        ),
        in_specs=[hbm] * 3,
        out_specs=(vmem, hbm),
        scratch_shapes=[
            pltpu.VMEM((NX * ROWS, D), BF16),
            pltpu.VMEM((NX * ROWS, D), BF16),
            pltpu.VMEM((D, NX * ROWS), BF16),
            pltpu.VMEM((D, COLS), BF16),
            pltpu.VMEM((ROWS, COLS), F32),
            pltpu.VMEM((ITERS, 3, 4, 16, 128), F32),
            pltpu.VMEM((ITERS, 2, 4, 3, 16, 128), F32),
            pltpu.VMEM((8, COLS), F32),
            pltpu.VMEM((5, 8, 128), F32),
            pltpu.VMEM((5, NP, 8, 128), F32),
            pltpu.VMEM((8, 128), F32),
            pltpu.VMEM((2, NX, 8, 128), F32),
            pltpu.VMEM((NX * NP, 8, 128), F32),
            pltpu.VMEM((NP, 3, 2, 128, D), F32),
            pltpu.VMEM((2, 2, 128, D), F32),
            pltpu.VMEM((NX, ROWS, 128), F32),
            pltpu.VMEM((NX * ROWS, CH), BF16),
            pltpu.VMEM((NQ, 2, 3, 32, CH), F32),
            pltpu.VMEM((NQ, 64, CH), F32),
            dma((6,)),
            dma, dma((ITERS, 2, 4)),
            dma((5,)), dma((5,)),
            dma((2, 4)), dma((2, 4)),
            dma((3, 2)), dma((3, 2)),
            dma((4,)), dma((4,)),
            dma, dma,
            dma, dma,
            dma, dma((NQ, 2, 3)),
            dma, dma, dma,
        ],
        compiler_params=pltpu.CompilerParams(
            collective_id=0, has_side_effects=True, vmem_limit_bytes=63 * 1024 * 1024
        ),
    )(teacher_emb, student_emb, prototypes)
    loss, grad = pl.pallas_call(
        handover,
        out_shape=(
            jax.ShapeDtypeStruct((8, 128), F32),
            jax.ShapeDtypeStruct((16, COLS), F32),
        ),
        in_specs=[vmem] * 2,
        out_specs=(vmem, vmem),
    )(loss, grad)
    return loss.reshape(ROWS), grad


def solution(mesh):
    in_specs = (P("batch", None), P("batch", None), P(None, "proto"))
    out_specs = (P("batch"), P("batch", "proto"))
    return jax.shard_map(local, mesh=mesh, in_specs=in_specs, out_specs=out_specs, check_vma=False)
```

```python
import jax
import jax.numpy as jnp
from jax import lax
from jax.experimental import pallas as pl
from jax.experimental.pallas import tpu as pltpu
from jax.sharding import PartitionSpec as P

PROTOS = 65536
CROPS = 16384
ITERS = 3
TEACHER_TEMP = 0.07
STUDENT_TEMP = 0.1
NP = 8
NX = 4
ROWS = 1024
COLS = 8192
D = 256
MINE = COLS // NX
CH = 256
NQ = MINE // CH
LAG = 3
FACTOR = PROTOS / (STUDENT_TEMP * CROPS)
CROSS = 1.0 / STUDENT_TEMP
LOG2E = 1.4426950408889634
MESH = pl.DeviceIdType.MESH
F32 = jnp.float32
BF16 = jnp.bfloat16


def unit(values, axis):
    wide = values.astype(F32)
    return (wide * lax.rsqrt(jnp.sum(wide * wide, axis=axis, keepdims=True) + 1e-06)).astype(BF16)


def rows_to_vec(part):
    out = []
    for i in range(8):
        block = part[pl.ds(i * 128, 128), :]
        out.append(jnp.sum(block.T, axis=0, keepdims=True))
    return jnp.concatenate(out, axis=0)


def vec_to_rows(vec, out):
    for i in range(8):
        out[pl.ds(i * 128, 128), :] = jnp.broadcast_to(vec[i : i + 1, :], (128, 128)).T


def send(src, dst, s, r, **where):
    pltpu.make_async_remote_copy(
        src_ref=src, dst_ref=dst, send_sem=s, recv_sem=r, device_id=where, device_id_type=MESH
    ).start()


def wait(some, sem):
    pltpu.make_async_copy(some, some, sem).wait()


def kernel(
    te, se, pr, loss, grad,
    ut, us, ust, up, big, colv, cin, cb, rvec, row_in, az, az_in, row_all,
    land, mine, pz, gb, ring, tot,
    s_in, s_col, r_col, s_row, r_row, s_x, r_x, s_z, r_z, s_k, r_k, s_az, r_az, s_all, r_all,
    s_ring, r_ring, s_out, r_out, s_own,
):
    mb = lax.axis_index("batch")
    mp = lax.axis_index("proto")
    y, x = mb // NX, lax.rem(mb, NX)
    other = mp + 1 - 2 * lax.rem(mp, 2)
    ut0, us0 = gb.at[pl.ds(0, ROWS), pl.ds(0, D)], gb.at[pl.ds(ROWS, ROWS), pl.ds(0, D)]
    wide, part, xp = pz.at[1], pz.at[2], pz.at[3]

    def at_x(d):
        return y * NX + lax.rem(x + d, NX)

    def at_y(d):
        return lax.rem(y + d, 4) * NX + x

    def at_z(d):
        return lax.rem(mp + 2 * d, NP)

    fetch = [pltpu.make_async_copy(te, ut0, s_in.at[0]), pltpu.make_async_copy(se, us0, s_in.at[1])]
    for j in range(4):
        cols = pl.ds(j * 2048, 2048)
        fetch.append(pltpu.make_async_copy(pr.at[:, cols], up.at[:, cols], s_in.at[2 + j]))
    for copy in fetch:
        copy.start()
    barrier = pltpu.get_barrier_semaphore()
    for d in (1, 2, 3):
        pl.semaphore_signal(barrier, inc=1, device_id={"batch": at_y(d)}, device_id_type=MESH)

    def greet(i, carry):
        there = {"batch": at_x(i // NP), "proto": lax.rem(mp + i, NP)}
        pl.semaphore_signal(barrier, inc=1, device_id=there, device_id_type=MESH)
        return carry

    lax.fori_loop(1, NX * NP, greet, 0)

    fetch[0].wait()
    ut0[...] = unit(ut0[...], 1)
    fetch[1].wait()
    us0[...] = unit(us0[...], 1)
    slab = pl.ds(pl.multiple_of(mp * 128, 128), 128)
    mine[0, 0] = ut0[slab, :].astype(F32)
    mine[0, 1] = us0[slab, :].astype(F32)
    def x_near(i, p):
        send(mine.at[i], land.at[p, 2], s_x.at[i, 0], r_x.at[i, 0], batch=at_x(1))
        send(mine.at[i], land.at[p, 0], s_x.at[i, 1], r_x.at[i, 1], batch=at_x(3))

    def x_far(i, p):
        wait(mine.at[0], r_x.at[i, 0])
        wait(mine.at[0], r_x.at[i, 1])
        send(land.at[p, 2, 0], land.at[p, 1, 0], s_x.at[i, 2], r_x.at[i, 2], batch=at_x(1))
        send(land.at[p, 0, 1], land.at[p, 1, 1], s_x.at[i, 3], r_x.at[i, 3], batch=at_x(3))

    def x_done(i, p):
        wait(land.at[p, 1, 0], r_x.at[i, 2])
        wait(land.at[p, 1, 1], r_x.at[i, 3])


    def col_send(it, ph, k):
        for d in (2, 1, 3):
            to = at_x(d) if ph else at_y(d)
            send(colv.at[it, ph, k], cin.at[it, ph, k, d - 1], s_col, r_col.at[it, ph, k], batch=to)

    def col_recv(it, ph, k):
        wait(cin.at[it, ph, k], r_col.at[it, ph, k])
        colv[it, ph + 1, k] = colv[it, ph, k] + cin[it, ph, k, 0] + cin[it, ph, k, 1] + cin[it, ph, k, 2]

    def first(j, carry):
        cols = pl.ds(pl.multiple_of(j * 2048, 2048), 2048)
        pltpu.make_async_copy(pr.at[:, cols], up.at[:, cols], s_in.at[2 + j]).wait()
        for k in range(4):
            some = pl.ds(pl.multiple_of(j * 2048 + k * 512, 512), 512)
            up[:, some] = unit(up[:, some], 0)
        w = up[:, cols]
        total = jnp.zeros((8, 2048), F32)
        for i in range(8):
            rows = pl.ds(i * 128, 128)
            e = jnp.exp2(jnp.dot(ut0[rows, :], w, preferred_element_type=F32) * (LOG2E / TEACHER_TEMP))
            big[rows, cols] = e
            total = total + jnp.sum(e.reshape(16, 8, 2048), axis=0)
        flat = jnp.sum(total, axis=0, keepdims=True)
        for k in range(16):
            colv[0, 0, j, pl.ds(k, 1), :] = flat[:, k * 128 : (k + 1) * 128]
        @pl.when(j == 0)
        def _():
            pl.semaphore_wait(barrier, 3 + NX * NP - 1)
            x_near(0, mp)

        col_send(0, 0, j)
        return carry

    lax.fori_loop(0, 4, first, 0)

    def row_pass(it, g):
        v = 1.0 / (colv[it, 2, g] * PROTOS)
        for j in range(16):
            cb[:, pl.ds((g * 16 + j) * 128, 128)] = jnp.broadcast_to(v[j : j + 1, :], (8, 128))
        c = [cb[:, pl.ds((g * 16 + k) * 128, 128)] for k in range(16)]

        def step(i, carry):
            res = []
            for u in range(16):
                rows = pl.ds(pl.multiple_of(i * 128, 128) + u * 8, 8)
                acc = [big[rows, pl.ds(g * 2048 + k * 128, 128)] * c[k] for k in range(4)]
                for k in range(4, 16):
                    acc[k % 4] = acc[k % 4] + big[rows, pl.ds(g * 2048 + k * 128, 128)] * c[k]
                total = (acc[0] + acc[1]) + (acc[2] + acc[3])
                res.append(total if g == 0 else part[rows, :] + total)
            for u in range(16):
                part[pl.ds(pl.multiple_of(i * 128, 128) + u * 8, 8), :] = res[u]
            return carry

        lax.fori_loop(0, 8, step, 0)

    def col_pass(it):
        for g in range(4):
            def step(i, acc):
                acc = list(acc)
                for u in range(4):
                    rows = pl.ds(pl.multiple_of(i * 32, 32) + u * 8, 8)
                    a = wide[rows, :]
                    for k in range(16):
                        acc[k] = acc[k] + big[rows, pl.ds(g * 2048 + k * 128, 128)] * a
                return tuple(acc)

            acc = lax.fori_loop(0, 32, step, tuple(jnp.zeros((8, 128), F32) for _ in range(16)))
            for k in range(16):
                colv[it, 0, g, pl.ds(k, 1), :] = jnp.sum(acc[k], axis=0, keepdims=True)
            col_send(it, 0, g)

    def row_send(src, dst, k):
        for d in (4, 3, 5, 2, 6, 7, 1):
            send(src, dst.at[mp], s_row.at[k], r_row.at[k], proto=lax.rem(mp + d, NP))

    def row_recv(src, dst, k):
        dst[mp] = src[...]
        wait(dst.at[pl.ds(0, NP - 1)], r_row.at[k])
        return jnp.sum(dst[...], axis=0)

    def student(lo, hi):
        def step(r, carry):
            rows = pl.ds(pl.multiple_of(r * 256, 256), 256)
            acc = jnp.zeros((256, 128), F32)
            for j in range(16):
                s = jnp.dot(us0[rows, :], up[:, pl.ds(j * 512, 512)], preferred_element_type=F32)
                e = jnp.exp2(s * (LOG2E / STUDENT_TEMP))
                for k in range(4):
                    acc = acc + e[:, k * 128 : (k + 1) * 128]
            xp[rows, :] = acc
            return carry

        lax.fori_loop(lo, hi, step, 0)

    def cross(r):
        rows = pl.ds(pl.multiple_of(r * 256, 256), 256)
        v = jnp.zeros((256, D), F32)
        for g in range(4):
            cols = pl.ds(g * 2048, 2048)
            kc = (big[rows, cols] * cb[pl.ds(0, 1), cols]).astype(BF16)
            v = v + lax.dot_general(kc, up[:, cols], (((1,), (1,)), ((), ())), preferred_element_type=F32)
        v = v * mine_us(r)
        v = v[:, :128] + v[:, 128:]
        for i in range(2):
            rvec[4, pl.ds(2 * r + i, 1), :] = jnp.sum(v[i * 128 : (i + 1) * 128].T, axis=0, keepdims=True)

    def mine_us(r):
        own = [us[pl.ds(pl.multiple_of((2 * r + i) * 512, 512), 128), :] for i in range(2)]
        return jnp.concatenate(own, axis=0).astype(F32)

    def slabs(p):
        for d in (1, 2, 3):
            rows = pl.ds(pl.multiple_of(p * 512, 512) + d * 128, 128)
            cols = pl.ds(pl.multiple_of(p * 512 + d * 128, 128), 128)
            ut[rows, :] = land[p, d - 1, 0].astype(BF16)
            v = land[p, d - 1, 1]
            us[rows, :] = v.astype(BF16)
            ust[:, cols] = v.T.astype(BF16)

    z1, z3, z2 = at_z(1), at_z(3), at_z(2)

    for k in range(2):
        col_recv(0, 0, k)
        col_send(0, 1, k)
    student(0, 2)
    for k in (2, 3):
        col_recv(0, 0, k)
        col_send(0, 1, k)
    x_far(0, mp)
    for k in range(4):
        col_recv(0, 1, k)
        row_pass(0, k)
    rvec[0] = rows_to_vec(part)
    row_send(rvec.at[0], row_in.at[0], 0)
    x_done(0, mp)
    most = pl.ds(0, 2)
    for k, to in ((0, z1), (1, z3)):
        send(land.at[mp, :, 0], land.at[mp, :, 0], s_z.at[0, k], r_z.at[0, k], proto=to)
    for k, to in ((0, z1), (1, z3)):
        send(land.at[mp, most, 1], land.at[mp, most, 1], s_z.at[1, k], r_z.at[1, k], proto=to)
    send(land.at[mp], land.at[mp], s_k.at[0], r_k.at[0], proto=other)
    slab = pl.ds(pl.multiple_of(z2 * 128, 128), 128)
    mine[1, 0] = ut0[slab, :].astype(F32)
    mine[1, 1] = us0[slab, :].astype(F32)
    x_near(1, z2)
    student(2, 4)
    rvec[3] = rows_to_vec(xp)
    total = row_recv(rvec.at[0], row_in.at[0], 0)
    vec_to_rows(1.0 / (total * CROPS), wide)

    col_pass(1)
    for i in range(8):
        v = us0[pl.ds(i * 128, 128), :]
        us[pl.ds(i * 512, 128), :] = v
        ust[:, pl.ds(i * 512, 128)] = v.astype(F32).T.astype(BF16)
        ut[pl.ds(i * 512, 128), :] = ut0[pl.ds(i * 128, 128), :]
    slabs(mp)
    for k in range(4):
        col_recv(1, 0, k)
        col_send(1, 1, k)
    for k in range(4):
        col_recv(1, 1, k)
        row_pass(1, k)
    rvec[1] = rows_to_vec(part)
    row_send(rvec.at[1], row_in.at[1], 1)
    row_send(rvec.at[3], row_in.at[3], 3)
    for k, to in ((0, z1), (1, z3)):
        send(land.at[mp, 2, 1], land.at[mp, 2, 1], s_z.at[2, k], r_z.at[2, k], proto=to)
    x_far(1, z2)
    wait(land.at[other], r_k.at[0])
    slabs(other)
    total = row_recv(rvec.at[1], row_in.at[1], 1)
    vec_to_rows(1.0 / (total * CROPS), wide)

    col_pass(2)
    z = row_recv(rvec.at[3], row_in.at[3], 3)
    az[...] = FACTOR / z
    for d in (1, 2, 3):
        send(az, az_in.at[0, 3 - d], s_az, r_az, batch=at_x(d))
    for k in range(2):
        wait(land.at[mp, :, 0], r_z.at[0, k])
        wait(land.at[mp, most, 1], r_z.at[1, k])
        wait(land.at[mp, 2, 1], r_z.at[2, k])
    x_done(1, z2)
    for k, p in ((1, z1), (2, z3), (3, z2)):
        send(land.at[p], land.at[p], s_k.at[k], r_k.at[k], proto=other)
    for k in range(4):
        col_recv(2, 0, k)
        col_send(2, 1, k)
    wait(az_in.at[0, pl.ds(0, 3)], r_az)
    vec_to_rows(az[...], pz.at[0])
    vec_to_rows(az_in[0, 0], pz.at[1])
    vec_to_rows(az_in[0, 2], pz.at[3])
    for k in range(4):
        col_recv(2, 1, k)
        row_pass(2, k)
    rvec[2] = rows_to_vec(part)

    def to_all(i, carry):
        e = i // NP
        there = lax.rem(mp + i, NP)
        pltpu.make_async_remote_copy(
            src_ref=rvec.at[2], dst_ref=row_all.at[lax.rem(NX - e, NX) * NP + mp], send_sem=s_all, recv_sem=r_all,
            device_id={"batch": at_x(e), "proto": there}, device_id_type=MESH,
        ).start()
        return carry

    lax.fori_loop(1, NX * NP, to_all, 0)
    row_all[mp] = rvec[2]
    slabs(z1)
    slabs(z3)
    slabs(z2)
    for k, p in ((1, z1), (2, z3), (3, z2)):
        theirs = p + 1 - 2 * lax.rem(p, 2)
        wait(land.at[theirs], r_k.at[k])
        slabs(theirs)
    vec_to_rows(az_in[0, 1], pz.at[2])

    def early(r, carry):
        cross(r)
        return carry

    lax.fori_loop(0, 2, early, 0)
    for k in range(4):
        wait(land.at[mp], s_k.at[k])
    for k in range(2):
        wait(land.at[mp, :, 0], s_z.at[0, k])
        wait(land.at[mp, most, 1], s_z.at[1, k])
        wait(land.at[mp, 2, 1], s_z.at[2, k])
        for i in range(2):
            wait(mine.at[0, 0], s_x.at[i, 2 + k])
    wait(row_all.at[pl.ds(0, NX * NP - 1)], r_all)
    for d in range(NX):
        az_in[1, d] = FACTOR / jnp.sum(row_all[pl.ds(d * NP, NP)], axis=0)

    base = x * MINE

    def block(q):
        cols = pl.ds(pl.multiple_of(base + q * CH, CH), CH)
        w = up[:, cols]
        c = cb[pl.ds(0, 1), cols]
        n = CH // 128
        for p in range(8):
            rows = pl.ds(p * 512, 512)
            own = pl.ds(p * 128, 128)
            s = jnp.dot(us[rows, :], w, preferred_element_type=F32)
            t = jnp.dot(ut[rows, :], w, preferred_element_type=F32)
            a = [jnp.broadcast_to(az_in[1, d, p : p + 1, :], (128, 128)).T for d in range(4)]
            a = jnp.concatenate(a, axis=0)
            e = jnp.concatenate([pz[d, own, :] for d in range(4)], axis=0)
            t = jnp.exp2(t * (LOG2E / TEACHER_TEMP)) * jnp.concatenate([a] * n, axis=1) * c
            s = jnp.exp2(s * (LOG2E / STUDENT_TEMP)) * jnp.concatenate([e] * n, axis=1)
            gb[rows, :] = (s - t).astype(BF16)
        g = jnp.dot(ust[...], gb[...], preferred_element_type=F32)
        land[q, 0, 0] = g[:128]
        land[q, 0, 1] = g[128:]

    def part_of(q, h, d):
        to = lax.rem(y + d, 4)
        return land.at[q, 0, to // 2, pl.ds(pl.multiple_of(lax.rem(to, 2) * 64 + h * 32, 32), 32)]

    def ring_first(q):
        for h in range(2):
            near, far = (1, 3) if h == 0 else (3, 1)
            send(part_of(q, h, 2), ring.at[q, h, 0], s_ring, r_ring.at[q, h, 0], batch=at_y(far))
            send(part_of(q, h, near), ring.at[q, h, 1], s_ring, r_ring.at[q, h, 1], batch=at_y(near))

    def ring_second(q):
        for h in range(2):
            far = 3 if h == 0 else 1
            wait(ring.at[q, h, 0], r_ring.at[q, h, 0])
            ring[q, h, 0] = ring[q, h, 0] + part_of(q, h, far)[...]
            send(ring.at[q, h, 0], ring.at[q, h, 2], s_ring, r_ring.at[q, h, 2], batch=at_y(far))

    def ring_last(q):
        for h in range(2):
            wait(ring.at[q, h, 1], r_ring.at[q, h, 1])
            wait(ring.at[q, h, 2], r_ring.at[q, h, 2])
            tot[q, pl.ds(h * 32, 32)] = part_of(q, h, 0)[...] + ring[q, h, 1] + ring[q, h, 2]
        cols = pl.ds(pl.multiple_of(base + q * CH, CH), CH)
        for d in (2, 1, 3):
            to = pl.ds(pl.multiple_of(lax.rem(x + d, NX) * 16, 16), 16)
            send(tot.at[q, to], grad.at[:, cols], s_out, r_out, batch=at_x(d))
        pltpu.make_async_copy(tot.at[q, pl.ds(pl.multiple_of(x * 16, 16), 16)], grad.at[:, cols], s_own).start()

    def last(q, carry):
        @pl.when(q < NQ)
        def _():
            block(q)
            ring_first(q)

        @pl.when((q >= LAG) & (q < NQ + LAG))
        def _():
            ring_second(q - LAG)

        @pl.when(q >= LAG + 4)
        def _():
            ring_last(q - LAG - 4)

        @pl.when((q >= NQ) & (q < NQ + 2))
        def _():
            cross(q - NQ + 2)

        @pl.when(q == NQ + 1)
        def _():
            rvec[4] = rvec[4] * CROSS / jnp.sum(row_all[pl.ds(0, NP)], axis=0)
            row_send(rvec.at[4], row_in.at[4], 4)

        return carry

    lax.fori_loop(0, NQ + LAG + 4, last, 0)
    loss[...] = jnp.log(z) - row_recv(rvec.at[4], row_in.at[4], 4)

    wait(grad.at[:, pl.ds(0, 3 * MINE)], r_out)
    wait(grad.at[:, pl.ds(0, 3 * MINE)], s_out)
    wait(grad.at[:, pl.ds(0, MINE)], s_own)
    wait(cin, s_col)
    for k in (0, 1, 3, 4):
        wait(row_in.at[k, pl.ds(0, NP - 1)], s_row.at[k])
    for i in range(2):
        for k in range(2):
            wait(mine.at[0], s_x.at[i, k])
    wait(az_in.at[0, pl.ds(0, 3)], s_az)
    wait(row_all.at[pl.ds(0, NX * NP - 1)], s_all)
    wait(ring, s_ring)


def handover(loss, grad, loss_out, grad_out, small, large, sems):
    def pieces(k):
        cols = pl.ds(k * 2048, 2048)
        return grad.at[:, cols], large.at[k], grad_out.at[:, cols]

    into = [pltpu.make_async_copy(pieces(k)[0], large.at[k], sems.at[0, k]) for k in range(4)]
    into.append(pltpu.make_async_copy(loss, small, sems.at[0, 4]))
    out = [pltpu.make_async_copy(large.at[k], pieces(k)[2], sems.at[1, k]) for k in range(4)]
    out.append(pltpu.make_async_copy(small, loss_out, sems.at[1, 4]))
    for copy in into:
        copy.start()
    for k in range(5):
        into[k].wait()
        out[k].start()
    for copy in out:
        copy.wait()


def local(teacher_emb, student_emb, prototypes):
    vmem = pl.BlockSpec(memory_space=pltpu.VMEM)
    hbm = pl.BlockSpec(memory_space=pl.ANY)
    dma = pltpu.SemaphoreType.DMA
    loss, grad = pl.pallas_call(
        kernel,
        out_shape=(
            jax.ShapeDtypeStruct((8, 128), F32),
            jax.ShapeDtypeStruct((16, COLS), F32),
        ),
        in_specs=[hbm] * 3,
        out_specs=(vmem, hbm),
        scratch_shapes=[
            pltpu.VMEM((NX * ROWS, D), BF16),
            pltpu.VMEM((NX * ROWS, D), BF16),
            pltpu.VMEM((D, NX * ROWS), BF16),
            pltpu.VMEM((D, COLS), BF16),
            pltpu.VMEM((ROWS, COLS), F32),
            pltpu.VMEM((ITERS, 3, 4, 16, 128), F32),
            pltpu.VMEM((ITERS, 2, 4, 3, 16, 128), F32),
            pltpu.VMEM((8, COLS), F32),
            pltpu.VMEM((5, 8, 128), F32),
            pltpu.VMEM((5, NP, 8, 128), F32),
            pltpu.VMEM((8, 128), F32),
            pltpu.VMEM((2, NX, 8, 128), F32),
            pltpu.VMEM((NX * NP, 8, 128), F32),
            pltpu.VMEM((NP, 3, 2, 128, D), F32),
            pltpu.VMEM((2, 2, 128, D), F32),
            pltpu.VMEM((NX, ROWS, 128), F32),
            pltpu.VMEM((NX * ROWS, CH), BF16),
            pltpu.VMEM((NQ, 2, 3, 32, CH), F32),
            pltpu.VMEM((NQ, 64, CH), F32),
            dma((6,)),
            dma, dma((ITERS, 2, 4)),
            dma((5,)), dma((5,)),
            dma((2, 4)), dma((2, 4)),
            dma((3, 2)), dma((3, 2)),
            dma((4,)), dma((4,)),
            dma, dma,
            dma, dma,
            dma, dma((NQ, 2, 3)),
            dma, dma, dma,
        ],
        compiler_params=pltpu.CompilerParams(
            collective_id=0, has_side_effects=True, vmem_limit_bytes=63 * 1024 * 1024
        ),
    )(teacher_emb, student_emb, prototypes)
    loss, grad = pl.pallas_call(
        handover,
        out_shape=(
            jax.ShapeDtypeStruct((8, 128), F32),
            jax.ShapeDtypeStruct((16, COLS), F32),
        ),
        in_specs=[hbm] * 2,
        out_specs=(hbm, hbm),
        scratch_shapes=[pltpu.VMEM((8, 128), F32), pltpu.VMEM((4, 16, 2048), F32), dma((2, 5))],
    )(loss, grad)
    return loss.reshape(ROWS), grad


def solution(mesh):
    in_specs = (P("batch", None), P("batch", None), P(None, "proto"))
    out_specs = (P("batch"), P("batch", "proto"))
    return jax.shard_map(local, mesh=mesh, in_specs=in_specs, out_specs=out_specs, check_vma=False)
```
